256 devices in a mesh: grp: 8 (over y, core), spl: 32 (over x, z).
Axes of the slice: x: 4, y: 4, z: 8, core: 2. Of those that a mesh axis runs over, the one named last changes fastest.
Arguments:
- slater: float32 [80, 5, 128, 128], P('grp', None, 'spl'), may hold values from -6 to 6
- couple_type: int32 [16384, 8], P('grp'), may hold values from 0 to 79
- couple_multipole: int32 [16384, 8], P('grp'), may hold values from 0 to 4
- couple_angle: int32 [16384, 8], P('grp'), may hold values from 0 to 63
- angular: float32 [64], replicated, may hold values from -1 to 1
- owner_map: int32 [16384], P('grp'), may hold values from 0 to 31, as said below
Outputs:
- hamiltonian: float32 [32768, 128, 128], P(('grp', 'spl'))
The draws below stay inside these ranges and needn't reach their ends.
Inputs may be any that keep to these rules, and one draw needn't show every extreme that they name: `owner_map`: within each group of 2048 consecutive pairs, a quarter of the 32 owners are named by exactly 128 pairs, a quarter by exactly 64, and the other half by exactly 32; which owners and which pairs vary.
All inputs are finite; a program needn't handle non-finite values.
Results may differ from the reference program's by a relative error of at most 0.0003.
Values sent between devices are 32-bit elements; how exact they have to be, the bound alone decides.
No kernel may reach another device: no remote copies, remote signals or barrier semaphores. Data moves between devices by JAX's collectives and lax.ppermute only.
A program may use at most 128 MiB of HBM per device.

```python
import jax
import jax.numpy as jnp
import numpy as np
from jax import lax

NS = 128
K = 5
ENT = 8
NQ = 64
P_DEV = 64
CAP = 128
P_GROUP = 2048
PAIRS = 16384
RT = 80
SLOTS = 32768
N_GRP = 8
N_SPL = 32


def draw_owner_map(key, part):
    key = jax.random.fold_in(key, 17)
    quarter = N_SPL // 4
    loads = np.array([2 * P_DEV] * quarter + [P_DEV] * quarter + [P_DEV // 2] * (N_SPL - 2 * quarter))

    def one_group(subkey):
        first, second = jax.random.split(subkey)
        labels = jax.random.permutation(first, N_SPL).astype(jnp.int32)
        listed = jnp.repeat(labels, loads, total_repeat_length=N_SPL * P_DEV)
        return jax.random.permutation(second, listed)
    group_keys = jax.random.split(key, N_GRP)
    return jax.vmap(one_group)(group_keys).reshape(-1).astype(jnp.int32)


def with_ends(values, stream_key, low, largest):
    longest = values.shape.index(max(values.shape))
    spots = []
    for shift in (0, 1):
        where = [jax.random.randint(jax.random.fold_in(stream_key, axis), (), 0, length) for axis, length in enumerate(values.shape)]
        where[longest] = (where[longest] + shift) % values.shape[longest]
        spots.append(tuple(where))
    return values.at[spots[0]].set(low).at[spots[1]].set(largest)


def levels(stream_key, shape, pieces, least, high):
    def one(dim, blocks):
        heights = jax.random.uniform(jax.random.fold_in(jax.random.fold_in(stream_key, 6), dim), (blocks,), jnp.float32, least / len(pieces), high / len(pieces))
        return jnp.repeat(jnp.exp(heights), shape[dim] // blocks).reshape((-1,) + (1,) * (len(shape) - dim - 1))

    gain = one(*pieces[0])
    for cut in pieces[1:]:
        gain = gain * one(*cut)
    return gain


def centred(own_key, dims, deviation, limit, cuts=(), kind=jnp.bfloat16):
    values = jax.random.normal(own_key, dims, jnp.float32) * deviation
    if len(cuts) > 0:
        values = levels(own_key, dims, cuts, -0.22, 0.18) * values
    return jnp.clip(values, min=-limit, max=limit).astype(kind)


def setup_inputs(seed: int = 0) -> dict:
    key_list = jax.random.split(jax.random.key(seed), 7)
    slater = centred(key_list[0], (RT, K, NS, NS), 1.0, 6.0, ((0, 8), (2, 32)), jnp.float32)
    couple_type = with_ends(jax.random.randint(key_list[1], (PAIRS, ENT), 0, RT), jax.random.fold_in(key_list[1], 1), 0, RT - 1).astype(jnp.int32)
    couple_multipole = with_ends(jax.random.randint(key_list[2], (PAIRS, ENT), 0, K), jax.random.fold_in(key_list[2], 1), 0, K - 1).astype(jnp.int32)
    couple_angle = with_ends(jax.random.randint(key_list[3], (PAIRS, ENT), 0, NQ), jax.random.fold_in(key_list[3], 1), 0, NQ - 1).astype(jnp.int32)
    angular = jnp.clip(jax.random.uniform(key_list[4], (NQ,), jnp.float32, -1.0, 1.0), -1.0, 1.0)
    owner_map = draw_owner_map(jax.random.fold_in(key_list[6], 71), 0)
    return {"slater": slater, "couple_type": couple_type, "couple_multipole": couple_multipole, "couple_angle": couple_angle, "angular": angular, "owner_map": owner_map}


def coefficients(types, multipoles, angles, angular):
    column = types * K + multipoles
    table_ids = jnp.arange(angular.shape[0], dtype=jnp.int32)
    values = jnp.sum(jnp.where(angles[:, :, None] == table_ids, angular, 0.0), axis=-1)
    column_ids = jnp.arange(RT * K, dtype=jnp.int32)
    total = jnp.zeros((types.shape[0], RT * K), jnp.float32)
    for entry in range(column.shape[1]):
        total = total + jnp.where(column[:, entry, None] == column_ids, values[:, entry, None], 0.0)
    return total


def slot_index(owners):
    indicator = (owners[:, None] == jnp.arange(N_SPL, dtype=jnp.int32)).astype(jnp.int32)
    running = jnp.cumsum(indicator, axis=0)
    ranking = jnp.sum(indicator * running, axis=1) - 1
    return owners * CAP + ranking


def reference(slater, couple_type, couple_multipole, couple_angle, angular, owner_map):
    matrix = slater.reshape(RT * K, NS * NS)

    def one_group(group):
        def take_rows(source):
            return lax.dynamic_slice_in_dim(source, group * P_GROUP, P_GROUP, 0)

        mixing = coefficients(take_rows(couple_type), take_rows(couple_multipole), take_rows(couple_angle), angular)
        blocks = jnp.dot(mixing, matrix, precision=lax.Precision.HIGHEST, preferred_element_type=jnp.float32)
        slots = slot_index(take_rows(owner_map))
        return jnp.zeros((N_SPL * CAP, NS * NS), jnp.float32).at[slots].set(blocks)

    result = lax.map(one_group, jnp.arange(N_GRP, dtype=jnp.int32))
    return result.reshape(SLOTS, NS, NS)
```

```python
import functools

import jax
import jax.numpy as jnp
import numpy as np
from jax import lax
from jax.experimental import pallas as pl
from jax.experimental.pallas import tpu as pltpu
from jax.sharding import Mesh
from jax.sharding import PartitionSpec as P

NY, NC, NX, NZ = 4, 2, 4, 8
ROWS = 4
COLS = 50
CUTS = (18, 16, 16)
FLAT = tuple(ROWS * cut for cut in CUTS)
K = NY * NC * COLS
SLOTS = 128
NS = 128
F32, BF16 = jnp.float32, jnp.bfloat16


def column_table():
    table = np.zeros((NC, NY, K), np.int32)
    for core in range(NC):
        for y in range(NY):
            place, first = 0, 0
            for cut in CUTS:
                for half in range(NC):
                    for step in range(NY):
                        source = (y - step if core == 0 else y + step) % NY
                        for j in range(cut):
                            table[core, y, place] = 100 * source + COLS * half + first + j
                            place += 1
                first += cut
    return table


def shift(value, axis, step):
    n = lax.axis_size(axis)
    return lax.ppermute(value, axis, [(i, (i + step) % n) for i in range(n)])


def turn(value, axis, step):
    n = lax.axis_size(axis)
    pairs = []
    for c in range(NC):
        for i in range(n):
            j = (i + (step if c == 0 else -step)) % n
            pairs.append((i * NC + c, j * NC + c) if axis == "y" else (c * n + i, c * n + j))
    return lax.ppermute(value, ("y", "core") if axis == "y" else ("core", axis), pairs)


def swap_halves(flat):
    pairs = []
    for c in range(NC):
        for z in range(NZ):
            high = (z >> 1) & 1
            if c == high:
                pairs.append((c * NZ + z, c * NZ + z))
            else:
                pairs.append((c * NZ + z, high * NZ + (z ^ 2)))
    return lax.ppermute(flat, ("core", "z"), pairs)


def together(*values):
    return lax.optimization_barrier(values)


def mixing_kernel(owner_ref, kind_ref, pole_ref, angle_ref, angular_ref, columns_ref, place_ref, out_ref, away_ref):
    me = place_ref[0]
    pairs = owner_ref.shape[0] * owner_ref.shape[1]
    groups = pairs // 128
    mine = (owner_ref[...] == me).astype(F32)
    low = lax.broadcasted_iota(jnp.int32, (128, 128), 0)
    high = lax.broadcasted_iota(jnp.int32, (128, 128), 1)
    upper = (low <= high).astype(BF16)
    within = jnp.dot(mine.astype(BF16), upper, preferred_element_type=F32)
    totals = jnp.sum(mine, axis=1, keepdims=True)
    before = jnp.zeros((groups, 1), F32)
    row = lax.broadcasted_iota(jnp.int32, (groups, 1), 0)
    for j in range(groups - 1):
        before = before + jnp.where(row > j, totals[j : j + 1, :], 0.0)
    rank = jnp.where(mine > 0.0, within + before - 1.0, -1.0).astype(jnp.int32)
    slot = lax.broadcasted_iota(jnp.int32, (SLOTS, 128), 0)
    chosen = jnp.zeros((24, SLOTS), F32)
    for j in range(groups):
        span = pl.ds(j * 128, 128)
        listed = jnp.concatenate([kind_ref[:, span], pole_ref[:, span], angle_ref[:, span]], axis=0)
        selected = (rank[j : j + 1, :] == slot).astype(BF16)
        chosen = chosen + lax.dot_general(
            listed.astype(F32).astype(BF16),
            selected,
            (((1,), (1,)), ((), ())),
            preferred_element_type=F32,
        )
    count = jnp.sum(totals, axis=0, keepdims=True)
    filled = lax.broadcasted_iota(jnp.int32, (1, SLOTS), 1).astype(F32) < count
    chosen = chosen.astype(jnp.int32)
    here, there = columns_ref[0], columns_ref[1]
    table = lax.broadcasted_iota(jnp.int32, (angular_ref.shape[0], SLOTS), 0)
    total = jnp.zeros((K, SLOTS), F32)
    away = jnp.zeros((K, SLOTS), F32)
    for entry in range(8):
        wanted = chosen[entry : entry + 1, :] * 5 + chosen[8 + entry : 9 + entry, :]
        angle = chosen[16 + entry : 17 + entry, :]
        value = jnp.sum(jnp.where(table == angle, angular_ref[...], 0.0), axis=0, keepdims=True)
        value = jnp.where(filled, value, 0.0)
        total = total + jnp.where(here == wanted, value, 0.0)
        away = away + jnp.where(there == wanted, value, 0.0)
    pad = jnp.zeros((512 - K, SLOTS), F32)
    out_ref[...] = jnp.concatenate([total, pad], axis=0).T
    away_ref[...] = jnp.concatenate([away, pad], axis=0).T


def mixing(owner_map, kinds, poles, angles, angular, columns, position):
    vmem = pl.BlockSpec(memory_space=pltpu.VMEM)
    return pl.pallas_call(
        mixing_kernel,
        out_shape=(jax.ShapeDtypeStruct((SLOTS, 512), F32),) * 2,
        in_specs=[vmem] * 6 + [pl.BlockSpec(memory_space=pltpu.SMEM)],
        out_specs=(vmem, vmem),
        compiler_params=pltpu.CompilerParams(vmem_limit_bytes=16 << 20),
    )(
        owner_map.reshape(-1, 128),
        kinds.T,
        poles.T,
        angles.T,
        angular[:, None],
        columns[:, :, None],
        position[None],
    )


def product_kernel(step, fresh, *refs):
    where_ref, own_ref, other_ref = refs[:3]
    a_refs, b_refs, c_ref = refs[3:12], refs[12:19], refs[19]
    refs = refs[20:] if fresh else refs[21:]
    out_ref, send_ref, a_all, b_all, c_all, kept, given, sems, out_sems = refs
    z, tile = where_ref[0], where_ref[1]
    copies = []

    def start(source, target):
        copy = pltpu.make_async_copy(source, target, sems.at[len(copies)])
        copy.start()
        copies.append(copy)

    low = step < 2
    near = step if low else step - 2
    for n in range(7):
        start(a_refs[n].at[step], a_all.at[n])
    start(a_refs[7 if low else 8].at[near], a_all.at[7])
    start(b_refs[0].at[step], b_all.at[0])
    for n in range(3):
        start(b_refs[(1 if low else 4) + n].at[near], b_all.at[1 + n])
    start(c_ref, c_all)
    spot = [lax.rem(s - z + NZ + 3, NZ) for s in range(NZ)]

    mix = jnp.concatenate([own_ref[...], other_ref[...]], axis=0)
    mix_high = mix.astype(BF16)
    mix_low = (mix - mix_high.astype(F32)).astype(BF16)
    left = jnp.concatenate([mix_high, mix_low], axis=0)
    for copy in copies:
        copy.wait()

    a_run, b_run, c_run = NY * CUTS[0], CUTS[1], NY * CUTS[2]
    pad = jnp.zeros((512 - K, NS), F32)
    for q in range(2):
        for b in range(2):
            for first in (0, 2):
                highs, lows = [], []
                for r in (first, first + 1):
                    zs = [4 * q + 2 * half + b for half in range(2)]
                    pieces = [a_all[spot[s], pl.ds(r, a_run, stride=ROWS), :] for s in zs]
                    pieces += [b_all[y, spot[s], pl.ds(r, b_run, stride=ROWS), :] for s in zs for y in range(NY)]
                    pieces += [c_all[spot[s], pl.ds(r, c_run, stride=ROWS), :] for s in zs]
                    value = jnp.concatenate(pieces + [pad], axis=0)
                    high = value.astype(BF16)
                    highs.append(high)
                    lows.append((value - high.astype(F32)).astype(BF16))
                right_high = jnp.concatenate(highs, axis=1)
                right_low = jnp.concatenate(lows, axis=1)
                full = jnp.dot(left, right_high, preferred_element_type=F32)
                rest = jnp.dot(mix_high, right_low, preferred_element_type=F32)
                total = full[: 2 * SLOTS] + (full[2 * SLOTS :] + rest)
                for n in range(2):
                    lanes = slice(n * NS, (n + 1) * NS)
                    row = pl.ds(4 * b + first + n, SLOTS, stride=8)
                    kept[q, row, :] = total[:SLOTS, lanes]
                    given[q, row, :] = total[SLOTS:, lanes]
    last = []
    for q in range(2):
        rows = pl.ds(pl.multiple_of(8 * (tile + 2 * q), 8), 8)
        source = kept.at[q].reshape(SLOTS, 8, NS)
        last.append(pltpu.make_async_copy(source, out_ref.at[:, rows, :], out_sems.at[q]))
    last.append(pltpu.make_async_copy(given, send_ref, out_sems.at[2]))
    for copy in last:
        copy.start()
    for copy in last:
        copy.wait()


def product(step, where, own, other, a_parts, b_parts, c_part, out):
    vmem = pl.BlockSpec(memory_space=pltpu.VMEM)
    anywhere = pl.BlockSpec(memory_space=pl.ANY)
    fresh = out is None
    operands = [where, own, other, *a_parts, *b_parts, c_part] + ([] if fresh else [out])
    flops = 2 * 8 * 768 * 512 * 256
    return pl.pallas_call(
        functools.partial(product_kernel, step, fresh),
        out_shape=(
            jax.ShapeDtypeStruct((SLOTS, NS, NS), F32),
            jax.ShapeDtypeStruct((2, SLOTS * 8, NS), F32),
        ),
        in_specs=[pl.BlockSpec(memory_space=pltpu.SMEM), vmem, vmem] + [anywhere] * (len(operands) - 3),
        out_specs=(anywhere, anywhere),
        scratch_shapes=[
            pltpu.VMEM((NZ, NY * FLAT[0], NS), F32),
            pltpu.VMEM((NY, NZ, FLAT[1], NS), F32),
            pltpu.VMEM((NZ, NY * FLAT[2], NS), F32),
            pltpu.VMEM((2, SLOTS * 8, NS), F32),
            pltpu.VMEM((2, SLOTS * 8, NS), F32),
            pltpu.SemaphoreType.DMA((13,)),
            pltpu.SemaphoreType.DMA((3,)),
        ],
        input_output_aliases={} if fresh else {20: 0},
        compiler_params=pltpu.CompilerParams(vmem_limit_bytes=24 << 20),
        cost_estimate=pl.CostEstimate(flops=flops, bytes_accessed=8 << 20, transcendentals=0),
    )(*operands)


def place_kernel(where_ref, *refs):
    count = (len(refs) - 3)
    blocks, out_ref, sems = refs[:count], refs[-2], refs[-1]
    copies = []
    for n in range(count):
        for q in range(2):
            rows = pl.ds(pl.multiple_of(8 * (where_ref[n] + 2 * q), 8), 8)
            source = blocks[n].at[q].reshape(SLOTS, 8, NS)
            copies.append(pltpu.make_async_copy(source, out_ref.at[:, rows, :], sems.at[2 * n + q]))
    for copy in copies:
        copy.start()
    for copy in copies:
        copy.wait()


def place(where, blocks, out):
    anywhere = pl.BlockSpec(memory_space=pl.ANY)
    vmem = pl.BlockSpec(memory_space=pltpu.VMEM)
    count = len(blocks)
    return pl.pallas_call(
        place_kernel,
        out_shape=jax.ShapeDtypeStruct(out.shape, F32),
        in_specs=[pl.BlockSpec(memory_space=pltpu.SMEM)] + [vmem] * count + [anywhere],
        out_specs=anywhere,
        scratch_shapes=[pltpu.SemaphoreType.DMA((2 * count,))],
        input_output_aliases={count + 1: 0},
        compiler_params=pltpu.CompilerParams(vmem_limit_bytes=8 << 20),
        cost_estimate=pl.CostEstimate(flops=0, bytes_accessed=count << 21, transcendentals=0),
    )(jnp.stack(where).astype(jnp.int32), *blocks, out)


def body(slater, couple_type, couple_multipole, couple_angle, angular, owner_map):
    y, core, x, z = (lax.axis_index(name) for name in ("y", "core", "x", "z"))
    flat = swap_halves(slater.reshape(COLS * ROWS, NS))
    part_a, part_bc = flat[: FLAT[0]], flat[FLAT[0] :]

    tables = jnp.asarray(column_table())[:, y]
    tables = jnp.where(core == 0, tables, tables[::-1])
    own, away = mixing(owner_map, couple_type, couple_multipole, couple_angle, angular, tables, x * NZ + z)
    other = lax.ppermute(away, "core", [(0, 1), (1, 0)])

    p1, m1 = shift(part_bc, "z", 1), shift(part_bc, "z", -1)
    a_y = [part_a] + [turn(part_a, "y", n) for n in (1, 2, 3)]
    p1, m1, *a_y = together(p1, m1, *a_y)
    a_y = jnp.concatenate(a_y, axis=0)
    p2, m2, p4 = shift(p1, "z", 1), shift(m1, "z", -1), shift(part_bc, "z", 4)
    a1, a3 = turn(a_y, "x", 1), turn(a_y, "x", -1)
    p2, m2, p4, a1, a3 = together(p2, m2, p4, a1, a3)
    p3, m3 = shift(p2, "z", 1), shift(m2, "z", -1)
    half = a_y.shape[0] // 2
    a2 = turn(a1[:half], "x", 1), turn(a3[half:], "x", -1)
    p3, m3, *a2 = together(p3, m3, *a2)
    a_x = jnp.stack([a_y, a1, jnp.concatenate(a2, axis=0), a3])
    bc = jnp.stack([p3, p2, p1, part_bc, m1, m2, m3, p4])

    ahead, behind = [shift(a_x, "z", 1)], [shift(a_x, "z", -1)]
    b_x, c_y = [bc[:, : FLAT[1]]], [bc[:, FLAT[1] :]]
    for _ in range(3):
        forth = turn(b_x[-1], "x", 1), turn(c_y[-1], "y", 1)
        if len(b_x) < 3:
            forth = together(*forth)
        else:
            *forth, ahead[0], behind[0] = together(*forth, ahead[0], behind[0])
        b_x.append(forth[0])
        c_y.append(forth[1])
    b_x, c_parts = jnp.stack(b_x), [jnp.concatenate(c_y, axis=1)]

    b_parts, one, three = [b_x], [], []
    for part in (b_x[:2], b_x[2:]):
        ahead.append(shift(ahead[-1], "z", 1))
        behind.append(shift(behind[-1], "z", -1))
        one.append(turn(part, "y", 1))
        three.append(turn(part, "y", -1))
        c_parts.append(turn(c_parts[-1], "x", 1))
        ahead[-1], behind[-1], one[-1], three[-1], c_parts[-1] = together(
            ahead[-1], behind[-1], one[-1], three[-1], c_parts[-1]
        )
    far = [shift(ahead[-1][:2], "z", 1), shift(behind[-1][2:], "z", -1)]
    two = [turn(one[0], "y", 1), turn(three[1], "y", -1)]
    c_parts.append(turn(c_parts[-1], "x", 1))
    a_parts = ahead[::-1] + [a_x] + behind + far
    b_parts = [b_x, one[0], two[0], three[0], one[1], two[1], three[1]]

    out, received, places = None, [], []
    for step in range(NX):
        from_x = lax.rem(x + jnp.where(core == 0, NX - step, step), NX)
        where = jnp.stack([z, 4 * from_x + core]).astype(jnp.int32)
        out, given = product(step, where, own, other, a_parts, b_parts, c_parts[step], out)
        received.append(lax.ppermute(given, "core", [(0, 1), (1, 0)]))
        opposite = lax.rem(x + jnp.where(core == 0, step, NX - step), NX)
        places.append(4 * opposite + 1 - core)
    out = place(places[:3], received[:3], out)
    return place(places[3:], received[3:], out)


def solution(mesh):
    fine = Mesh(mesh.devices.reshape(NY, NC, NX, NZ), ("y", "core", "x", "z"))
    groups = ("y", "core")
    return jax.shard_map(
        body,
        mesh=fine,
        in_specs=(
            P(groups, None, ("x", "z"), None),
            P(groups, None),
            P(groups, None),
            P(groups, None),
            P(),
            P(groups),
        ),
        out_specs=P(("y", "core", "x", "z"), None, None),
        check_vma=False,
    )
```

```python
import functools

import jax
import jax.numpy as jnp
from jax import lax
from jax.experimental import pallas as pl
from jax.experimental.pallas import tpu as pltpu
from jax.sharding import Mesh
from jax.sharding import PartitionSpec as P

NY, NC, NX, NZ = 4, 2, 4, 8
ROWS = 4
COLS = 50
CUTS = (10, 18, 22)
FLAT = tuple(ROWS * cut for cut in CUTS)
K = NY * NC * COLS
SLOTS = 128
NS = 128
F32, BF16 = jnp.float32, jnp.bfloat16


def shift(value, axis, step):
    n = lax.axis_size(axis)
    return lax.ppermute(value, axis, [(i, (i + step) % n) for i in range(n)])


def turn(value, axis, step):
    n = lax.axis_size(axis)
    pairs = []
    for c in range(NC):
        for i in range(n):
            j = (i + (step if c == 0 else -step)) % n
            pairs.append((i * NC + c, j * NC + c) if axis == "y" else (c * n + i, c * n + j))
    return lax.ppermute(value, ("y", "core") if axis == "y" else ("core", axis), pairs)


def trade(value, axis, bit):
    n = lax.axis_size(axis)
    return lax.ppermute(value, axis, [(i, i ^ bit) for i in range(n)])


def swap_halves(flat):
    pairs = []
    for c in range(NC):
        for z in range(NZ):
            high = (z >> 1) & 1
            if c == high:
                pairs.append((c * NZ + z, c * NZ + z))
            else:
                pairs.append((c * NZ + z, high * NZ + (z ^ 2)))
    return lax.ppermute(flat, ("core", "z"), pairs)


def together(*values):
    return lax.optimization_barrier(values)


def global_columns(y):
    place = lax.broadcasted_iota(jnp.int32, (K, 1), 0)
    ids, start, offset, first = place, 0, 0, 0
    for part, cut in enumerate(CUTS):
        for half in range(NC):
            for step in range(NY):
                source = y ^ step if part == 0 else lax.rem(y + NY - step, NY)
                now = 100 * source + COLS * half + first - start
                ids = ids + jnp.where(place >= start, now - offset, 0)
                offset, start = now, start + cut
        first += cut
    return ids


def mixing_kernel(owner_ref, kind_ref, pole_ref, angle_ref, angular_ref, out_ref):
    me = lax.axis_index("x") * NZ + lax.axis_index("z")
    pairs = owner_ref.shape[0] * owner_ref.shape[1]
    groups = pairs // 128
    mine = (owner_ref[...] == me).astype(F32)
    low = lax.broadcasted_iota(jnp.int32, (128, 128), 0)
    high = lax.broadcasted_iota(jnp.int32, (128, 128), 1)
    upper = (low <= high).astype(BF16)
    within = jnp.dot(mine.astype(BF16), upper, preferred_element_type=F32)
    totals = jnp.sum(mine, axis=1, keepdims=True)
    before = jnp.zeros((groups, 1), F32)
    row = lax.broadcasted_iota(jnp.int32, (groups, 1), 0)
    for j in range(groups - 1):
        before = before + jnp.where(row > j, totals[j : j + 1, :], 0.0)
    rank = jnp.where(mine > 0.0, within + before - 1.0, -1.0).astype(jnp.int32)
    slot = lax.broadcasted_iota(jnp.int32, (SLOTS, 128), 0)
    chosen = jnp.zeros((24, SLOTS), F32)
    for j in range(groups):
        span = pl.ds(j * 128, 128)
        listed = jnp.concatenate([kind_ref[:, span], pole_ref[:, span], angle_ref[:, span]], axis=0)
        selected = (rank[j : j + 1, :] == slot).astype(BF16)
        chosen = chosen + lax.dot_general(
            listed.astype(F32).astype(BF16),
            selected,
            (((1,), (1,)), ((), ())),
            preferred_element_type=F32,
        )
    count = jnp.sum(totals, axis=0, keepdims=True)
    filled = lax.broadcasted_iota(jnp.int32, (1, SLOTS), 1).astype(F32) < count
    chosen = chosen.astype(jnp.int32)
    column = global_columns(lax.axis_index("y"))
    size = angular_ref.shape[1]
    table = lax.broadcasted_iota(jnp.int32, (size, SLOTS), 0)
    down, across = (lax.broadcasted_iota(jnp.int32, (size, size), d) for d in range(2))
    angular = jnp.sum(jnp.where(down == across, angular_ref[...], 0.0), axis=1, keepdims=True)
    total = jnp.zeros((K, SLOTS), F32)
    for entry in range(8):
        wanted = chosen[entry : entry + 1, :] * 5 + chosen[8 + entry : 9 + entry, :]
        angle = chosen[16 + entry : 17 + entry, :]
        value = jnp.sum(jnp.where(table == angle, angular, 0.0), axis=0, keepdims=True)
        value = jnp.where(filled, value, 0.0)
        total = total + jnp.where(column == wanted, value, 0.0)
    pad = jnp.zeros((512 - K, SLOTS), F32)
    out_ref[...] = jnp.concatenate([total, pad], axis=0).T


def mixing(owner_map, kinds, poles, angles, angular):
    vmem = pl.BlockSpec(memory_space=pltpu.VMEM)
    return pl.pallas_call(
        mixing_kernel,
        out_shape=jax.ShapeDtypeStruct((SLOTS, 512), F32),
        in_specs=[vmem] * 5,
        out_specs=vmem,
        compiler_params=pltpu.CompilerParams(vmem_limit_bytes=16 << 20),
        cost_estimate=pl.CostEstimate(flops=100 << 20, bytes_accessed=1 << 20, transcendentals=0),
    )(owner_map.reshape(-1, 128), kinds.T, poles.T, angles.T, angular[None, :])


def before(x, core, step):
    return lax.rem(x + jnp.where(core == 0, NX - step, step), NX)


def product_kernel(step, fresh, *refs):
    own_ref, other_ref = refs[:2]
    a_refs, b_refs, c_ref = refs[2:11], refs[11:16], refs[16]
    refs = refs[17:] if fresh else refs[18:]
    out_ref, send_ref, a_all, b_all, c_all, kept, given, sems, out_sems = refs
    core, x, z = (lax.axis_index(name) for name in ("core", "x", "z"))
    source_x = before(x, core, step)
    tile = 4 * source_x + core
    copies = []

    def start(source, target):
        copy = pltpu.make_async_copy(source, target, sems.at[len(copies)])
        copy.start()
        copies.append(copy)

    for n in range(7):
        start(a_refs[n].at[x ^ source_x], a_all.at[n])
    half = a_all.shape[1] // 2
    for n in range(2):
        start(a_refs[7 + n].at[x ^ source_x], a_all.at[7, pl.ds(n * half, half), :])
    start(b_refs[0].at[step], b_all.at[0])
    start(b_refs[1].at[step], b_all.at[1])
    start(b_refs[2 + step // 2].at[step % 2], b_all.at[2])
    start(b_refs[4].at[step], b_all.at[3])
    start(c_ref, c_all)
    spot = [lax.rem(s - z + NZ + 3, NZ) for s in range(NZ)]

    mix = jnp.concatenate([own_ref[...], other_ref[...]], axis=0)
    mix_high = mix.astype(BF16)
    mix_low = (mix - mix_high.astype(F32)).astype(BF16)
    left = jnp.concatenate([mix_high, mix_low], axis=0)
    for copy in copies:
        copy.wait()

    a_run, b_run, c_run = NY * CUTS[0], CUTS[1], NY * CUTS[2]
    pad = jnp.zeros((512 - K, NS), F32)
    for q in range(2):
        for b in range(2):
            for first in (0, 2):
                highs, lows = [], []
                for r in (first, first + 1):
                    zs = [4 * q + 2 * half + b for half in range(2)]
                    pieces = [a_all[spot[s], pl.ds(r, a_run, stride=ROWS), :] for s in zs]
                    pieces += [b_all[y, spot[s], pl.ds(r, b_run, stride=ROWS), :] for s in zs for y in range(NY)]
                    pieces += [c_all[spot[s], pl.ds(r, c_run, stride=ROWS), :] for s in zs]
                    value = jnp.concatenate(pieces + [pad], axis=0)
                    high = value.astype(BF16)
                    highs.append(high)
                    lows.append((value - high.astype(F32)).astype(BF16))
                right_high = jnp.concatenate(highs, axis=1)
                right_low = jnp.concatenate(lows, axis=1)
                full = jnp.dot(left, right_high, preferred_element_type=F32)
                rest = jnp.dot(mix_high, right_low, preferred_element_type=F32)
                total = full[: 2 * SLOTS] + (full[2 * SLOTS :] + rest)
                for n in range(2):
                    lanes = slice(n * NS, (n + 1) * NS)
                    row = pl.ds(4 * b + first + n, SLOTS, stride=8)
                    kept[q, row, :] = total[:SLOTS, lanes]
                    given[q, row, :] = total[SLOTS:, lanes]
    last = []
    for q in range(2):
        rows = pl.ds(pl.multiple_of(8 * (tile + 2 * q), 8), 8)
        source = kept.at[q].reshape(SLOTS, 8, NS)
        last.append(pltpu.make_async_copy(source, out_ref.at[:, rows, :], out_sems.at[q]))
    last.append(pltpu.make_async_copy(given, send_ref, out_sems.at[2]))
    for copy in last:
        copy.start()
    for copy in last:
        copy.wait()


def product(step, own, other, a_parts, b_parts, c_part, out):
    vmem = pl.BlockSpec(memory_space=pltpu.VMEM)
    anywhere = pl.BlockSpec(memory_space=pl.ANY)
    fresh = out is None
    operands = [own, other, *a_parts, *b_parts, c_part] + ([] if fresh else [out])
    flops = 2 * 8 * 768 * 512 * 256
    return pl.pallas_call(
        functools.partial(product_kernel, step, fresh),
        out_shape=(
            jax.ShapeDtypeStruct((SLOTS, NS, NS), F32),
            jax.ShapeDtypeStruct((2, SLOTS * 8, NS), F32),
        ),
        in_specs=[vmem, vmem] + [anywhere] * (len(operands) - 2),
        out_specs=(anywhere, anywhere),
        scratch_shapes=[
            pltpu.VMEM((NZ, NY * FLAT[0], NS), F32),
            pltpu.VMEM((NY, NZ, FLAT[1], NS), F32),
            pltpu.VMEM((NZ, NY * FLAT[2], NS), F32),
            pltpu.VMEM((2, SLOTS * 8, NS), F32),
            pltpu.VMEM((2, SLOTS * 8, NS), F32),
            pltpu.SemaphoreType.DMA((14,)),
            pltpu.SemaphoreType.DMA((3,)),
        ],
        input_output_aliases={} if fresh else {17: 0},
        compiler_params=pltpu.CompilerParams(vmem_limit_bytes=24 << 20),
        cost_estimate=pl.CostEstimate(flops=flops, bytes_accessed=8 << 20, transcendentals=0),
    )(*operands)


def place_kernel(steps, *refs):
    count = len(steps)
    blocks, out_ref, sems = refs[:count], refs[-2], refs[-1]
    core, x = lax.axis_index("core"), lax.axis_index("x")
    copies = []
    for n, step in enumerate(steps):
        tile = 4 * before(x, 1 - core, step) + 1 - core
        for q in range(2):
            rows = pl.ds(pl.multiple_of(8 * (tile + 2 * q), 8), 8)
            source = blocks[n].at[q].reshape(SLOTS, 8, NS)
            copies.append(pltpu.make_async_copy(source, out_ref.at[:, rows, :], sems.at[2 * n + q]))
    for copy in copies:
        copy.start()
    for copy in copies:
        copy.wait()


def place(steps, blocks, out):
    anywhere = pl.BlockSpec(memory_space=pl.ANY)
    vmem = pl.BlockSpec(memory_space=pltpu.VMEM)
    count = len(blocks)
    return pl.pallas_call(
        functools.partial(place_kernel, steps),
        out_shape=jax.ShapeDtypeStruct(out.shape, F32),
        in_specs=[vmem] * count + [anywhere],
        out_specs=anywhere,
        scratch_shapes=[pltpu.SemaphoreType.DMA((2 * count,))],
        input_output_aliases={count: 0},
        compiler_params=pltpu.CompilerParams(vmem_limit_bytes=8 << 20),
        cost_estimate=pl.CostEstimate(flops=0, bytes_accessed=count << 21, transcendentals=0),
    )(*blocks, out)


def body(slater, couple_type, couple_multipole, couple_angle, angular, owner_map):
    flat = swap_halves(slater.reshape(COLS * ROWS, NS))
    part_a, part_bc = flat[: FLAT[0]], flat[FLAT[0] :]

    p1, m1, p2, m2 = (shift(part_bc, "z", n) for n in (1, -1, 2, -2))
    a_y = jnp.concatenate([part_a, trade(part_a, "y", 1)], axis=0)
    p1, m1, p2, m2, a_y = together(p1, m1, p2, m2, a_y)
    p3, m3, p4 = shift(p2, "z", 1), shift(m2, "z", -1), shift(p2, "z", 2)
    a_y = jnp.concatenate([a_y, trade(a_y, "y", 2)], axis=0)
    p3, m3, p4, a_y = together(p3, m3, p4, a_y)
    bc = jnp.stack([p3, p2, p1, part_bc, m1, m2, m3, p4])

    b_0, c_0 = bc[:, : FLAT[1]], bc[:, FLAT[1] :]
    b_1, b_3 = turn(b_0, "x", 1), turn(b_0, "x", -1)
    c_1, c_3 = shift(c_0, "y", 1), shift(c_0, "y", -1)
    a_x = jnp.stack([a_y, trade(a_y, "x", 1)])
    b_1, b_3, c_1, c_3, a_x = together(b_1, b_3, c_1, c_3, a_x)
    b_2 = turn(b_1[:4], "x", 1), turn(b_3[4:], "x", -1)
    c_2 = shift(c_1[:4], "y", 1), shift(c_3[4:], "y", -1)
    a_x = jnp.concatenate([a_x, trade(a_x, "x", 2)], axis=0)
    *b_2, c_20, c_21, a_x = together(*b_2, *c_2, a_x)
    b_x = jnp.stack([b_0, b_1, jnp.concatenate(b_2, axis=0), b_3])
    c_y = jnp.concatenate([c_0, c_1, jnp.concatenate([c_20, c_21], axis=0), c_3], axis=1)

    up_1, down_1 = shift(a_x, "z", 1), shift(a_x, "z", -1)
    x_1 = turn(c_y, "x", 1)
    y_1, y_3 = shift(b_x, "y", 1), shift(b_x, "y", -1)
    up, down = together(up_1, down_1)
    up_2, down_2 = shift(up, "z", 1), shift(down, "z", -1)
    x_2 = turn(together(x_1, up_1, down_1)[0], "x", 1)
    up, down, _ = together(up_2, down_2, x_1)
    up_3, down_3 = shift(up, "z", 1), shift(down, "z", -1)
    up, down, _, _ = together(y_1, y_3, up_2, down_2)
    y_2 = shift(up[:2], "y", 1), shift(down[2:], "y", -1)
    x_3 = turn(together(x_2, up_3, down_3)[0], "x", 1)
    half = a_x.shape[1] // 2
    up, down, _, _ = together(up_3, down_3, y_1, y_3)
    far = shift(up[:, :half], "z", 1), shift(down[:, half:], "z", -1)

    own = mixing(owner_map, couple_type, couple_multipole, couple_angle, angular)
    other = lax.ppermute(own, "core", [(0, 1), (1, 0)])
    a_parts = [up_3, up_2, up_1, a_x, down_1, down_2, down_3, *far]
    b_parts = [b_x, y_1, *y_2, y_3]
    out, received = None, []
    for step, c_part in enumerate((c_y, x_1, x_2, x_3)):
        if step == 3:
            out = place((0, 1), received[:2], out)
        out, given = product(step, own, other, a_parts, b_parts, c_part, out)
        received.append(lax.ppermute(given, "core", [(0, 1), (1, 0)]))
    out = place((2,), received[2:3], out)
    return place((3,), received[3:], out)


def solution(mesh):
    fine = Mesh(mesh.devices.reshape(NY, NC, NX, NZ), ("y", "core", "x", "z"))
    groups = ("y", "core")
    return jax.shard_map(
        body,
        mesh=fine,
        in_specs=(
            P(groups, None, ("x", "z"), None),
            P(groups, None),
            P(groups, None),
            P(groups, None),
            P(),
            P(groups),
        ),
        out_specs=P(("y", "core", "x", "z"), None, None),
        check_vma=False,
    )
```

```python
import functools

import jax
import jax.numpy as jnp
from jax import lax
from jax.experimental import pallas as pl
from jax.experimental.pallas import tpu as pltpu
from jax.sharding import Mesh
from jax.sharding import PartitionSpec as P

NY, NC, NX, NZ = 4, 2, 4, 8
ROWS = 4
COLS = 50
CUTS = (10, 20, 20)
FLAT = tuple(ROWS * cut for cut in CUTS)
K = NY * NC * COLS
SLOTS = 128
NS = 128
F32, BF16 = jnp.float32, jnp.bfloat16


def shift(value, axis, step):
    n = lax.axis_size(axis)
    return lax.ppermute(value, axis, [(i, (i + step) % n) for i in range(n)])


def turn(value, axis, step):
    n = lax.axis_size(axis)
    pairs = []
    for c in range(NC):
        for i in range(n):
            j = (i + (step if c == 0 else -step)) % n
            pairs.append((i * NC + c, j * NC + c) if axis == "y" else (c * n + i, c * n + j))
    return lax.ppermute(value, ("y", "core") if axis == "y" else ("core", axis), pairs)


def trade(value, axis, bit):
    n = lax.axis_size(axis)
    return lax.ppermute(value, axis, [(i, i ^ bit) for i in range(n)])


def swap_halves(flat):
    pairs = []
    for c in range(NC):
        for z in range(NZ):
            high = (z >> 1) & 1
            if c == high:
                pairs.append((c * NZ + z, c * NZ + z))
            else:
                pairs.append((c * NZ + z, high * NZ + (z ^ 2)))
    return lax.ppermute(flat, ("core", "z"), pairs)


def together(*values):
    return lax.optimization_barrier(values)


def global_columns(y):
    place = lax.broadcasted_iota(jnp.int32, (K, 1), 0)
    ids, start, offset, first = place, 0, 0, 0
    for part, cut in enumerate(CUTS):
        for half in range(NC):
            for step in range(NY):
                source = y ^ step if part == 0 else lax.rem(y + NY - step, NY)
                now = 100 * source + COLS * half + first - start
                ids = ids + jnp.where(place >= start, now - offset, 0)
                offset, start = now, start + cut
        first += cut
    return ids


def mixing_kernel(owner_ref, kind_ref, pole_ref, angle_ref, angular_ref, out_ref):
    me = lax.axis_index("x") * NZ + lax.axis_index("z")
    pairs = owner_ref.shape[0] * owner_ref.shape[1]
    groups = pairs // 128
    mine = (owner_ref[...] == me).astype(F32)
    low = lax.broadcasted_iota(jnp.int32, (128, 128), 0)
    high = lax.broadcasted_iota(jnp.int32, (128, 128), 1)
    upper = (low <= high).astype(BF16)
    within = jnp.dot(mine.astype(BF16), upper, preferred_element_type=F32)
    totals = jnp.sum(mine, axis=1, keepdims=True)
    before = jnp.zeros((groups, 1), F32)
    row = lax.broadcasted_iota(jnp.int32, (groups, 1), 0)
    for j in range(groups - 1):
        before = before + jnp.where(row > j, totals[j : j + 1, :], 0.0)
    rank = jnp.where(mine > 0.0, within + before - 1.0, -1.0).astype(jnp.int32)
    slot = lax.broadcasted_iota(jnp.int32, (SLOTS, 128), 0)
    chosen = jnp.zeros((24, SLOTS), F32)
    for j in range(groups):
        span = pl.ds(j * 128, 128)
        listed = jnp.concatenate([kind_ref[:, span], pole_ref[:, span], angle_ref[:, span]], axis=0)
        selected = (rank[j : j + 1, :] == slot).astype(BF16)
        chosen = chosen + lax.dot_general(
            listed.astype(F32).astype(BF16),
            selected,
            (((1,), (1,)), ((), ())),
            preferred_element_type=F32,
        )
    count = jnp.sum(totals, axis=0, keepdims=True)
    filled = lax.broadcasted_iota(jnp.int32, (1, SLOTS), 1).astype(F32) < count
    chosen = chosen.astype(jnp.int32)
    column = global_columns(lax.axis_index("y"))
    size = angular_ref.shape[1]
    table = lax.broadcasted_iota(jnp.int32, (size, SLOTS), 0)
    down, across = (lax.broadcasted_iota(jnp.int32, (size, size), d) for d in range(2))
    angular = jnp.sum(jnp.where(down == across, angular_ref[...], 0.0), axis=1, keepdims=True)
    total = jnp.zeros((K, SLOTS), F32)
    for entry in range(8):
        wanted = chosen[entry : entry + 1, :] * 5 + chosen[8 + entry : 9 + entry, :]
        angle = chosen[16 + entry : 17 + entry, :]
        value = jnp.sum(jnp.where(table == angle, angular, 0.0), axis=0, keepdims=True)
        value = jnp.where(filled, value, 0.0)
        total = total + jnp.where(column == wanted, value, 0.0)
    pad = jnp.zeros((512 - K, SLOTS), F32)
    out_ref[...] = jnp.concatenate([total, pad], axis=0).T


def mixing(owner_map, kinds, poles, angles, angular):
    vmem = pl.BlockSpec(memory_space=pltpu.VMEM)
    return pl.pallas_call(
        mixing_kernel,
        out_shape=jax.ShapeDtypeStruct((SLOTS, 512), F32),
        in_specs=[vmem] * 5,
        out_specs=vmem,
        compiler_params=pltpu.CompilerParams(vmem_limit_bytes=16 << 20),
        cost_estimate=pl.CostEstimate(flops=100 << 20, bytes_accessed=1 << 20, transcendentals=0),
    )(owner_map.reshape(-1, 128), kinds.T, poles.T, angles.T, angular[None, :])


def before(x, core, step):
    return lax.rem(x + jnp.where(core == 0, NX - step, step), NX)


def product_kernel(steps, fresh, *refs):
    count = len(steps)
    own_ref, other_ref = refs[:2]
    a_ref, b_refs, c_refs = refs[2], refs[3:8], refs[8:13]
    refs = refs[13 + (0 if fresh else 1) :]
    out_ref, send_refs = refs[0], refs[1 : 1 + count]
    a_all, b_all, c_all, left_all, kept, given, sems, out_sems = refs[1 + count :]
    core, x, z = (lax.axis_index(name) for name in ("core", "x", "z"))

    def arrive(n):
        step = steps[n]
        copies = []

        def add(source, target):
            copies.append(pltpu.make_async_copy(source, target, sems.at[n, len(copies)]))

        add(a_ref.at[:, x ^ before(x, core, step)], a_all.at[n])
        add(b_refs[0].at[step], b_all.at[n, 0])
        add(b_refs[1].at[step], b_all.at[n, 1])
        add(b_refs[2 + step // 2].at[step % 2], b_all.at[n, 2])
        add(b_refs[4].at[step], b_all.at[n, 3])
        if step == 2:
            for half in range(2):
                add(c_refs[2 + half], c_all.at[n, pl.ds(4 * half, 4)])
        else:
            add(c_refs[(0, 1, None, 4)[step]], c_all.at[n])
        return copies

    def leave(n, q):
        rows = pl.ds(pl.multiple_of(8 * (4 * before(x, core, steps[n]) + core + 2 * q), 8), 8)
        return (
            pltpu.make_async_copy(
                kept.at[n, q].reshape(SLOTS, 8, NS), out_ref.at[:, rows, :], out_sems.at[n, q]
            ),
            pltpu.make_async_copy(given.at[n, q], send_refs[n].at[q], out_sems.at[n, 2 + q]),
        )

    for copy in arrive(0):
        copy.start()
    mix = jnp.concatenate([own_ref[...], other_ref[...]], axis=0)
    mix_high = mix.astype(BF16)
    left_all[: 2 * SLOTS, :] = mix_high
    left_all[2 * SLOTS :, :] = (mix - mix_high.astype(F32)).astype(BF16)
    a_run, b_run, c_run = NY * CUTS[0], CUTS[1], NY * CUTS[2]
    pad = jnp.zeros((512 - K, NS), F32)

    for n in range(count):
        for copy in arrive(n):
            copy.wait()
        if n + 1 < count:
            for copy in arrive(n + 1):
                copy.start()

        def one_tile(q, carry, n=n):
            for b in range(2):
                places = [4 * q + 2 * half + b for half in range(2)]
                spots = [lax.rem(place - z + NZ + 3, NZ) for place in places]
                for first in (0, 2):
                    highs, lows = [], []
                    for r in (first, first + 1):
                        pieces = [a_all[n, s, pl.ds(r, a_run, stride=ROWS), :] for s in places]
                        pieces += [
                            b_all[n, y, s, pl.ds(r, b_run, stride=ROWS), :] for s in spots for y in range(NY)
                        ]
                        pieces += [c_all[n, s, pl.ds(r, c_run, stride=ROWS), :] for s in spots]
                        value = jnp.concatenate(pieces + [pad], axis=0)
                        high = value.astype(BF16)
                        highs.append(high)
                        lows.append((value - high.astype(F32)).astype(BF16))
                    right_high = jnp.concatenate(highs, axis=1)
                    right_low = jnp.concatenate(lows, axis=1)
                    full = jnp.dot(left_all[...], right_high, preferred_element_type=F32)
                    rest = jnp.dot(left_all[: 2 * SLOTS, :], right_low, preferred_element_type=F32)
                    total = full[: 2 * SLOTS] + (full[2 * SLOTS :] + rest)
                    for m in range(2):
                        lanes = slice(m * NS, (m + 1) * NS)
                        row = pl.ds(4 * b + first + m, SLOTS, stride=8)
                        kept[n, q, row, :] = total[:SLOTS, lanes]
                        given[n, q, row, :] = total[SLOTS:, lanes]
            for copy in leave(n, q):
                copy.start()
            return carry

        lax.fori_loop(0, 2, one_tile, 0)
    for n in range(count):
        for q in range(2):
            for copy in leave(n, q):
                copy.wait()


def product(steps, own, other, a_part, b_parts, c_parts, out):
    vmem = pl.BlockSpec(memory_space=pltpu.VMEM)
    anywhere = pl.BlockSpec(memory_space=pl.ANY)
    hbm = pl.BlockSpec(memory_space=pltpu.HBM)
    fresh, count = out is None, len(steps)
    operands = [own, other, a_part, *b_parts, *c_parts] + ([] if fresh else [out])
    flops = 2 * 8 * 768 * 512 * 256
    return pl.pallas_call(
        functools.partial(product_kernel, steps, fresh),
        out_shape=(
            jax.ShapeDtypeStruct((SLOTS, NS, NS), F32),
            *[jax.ShapeDtypeStruct((2, SLOTS * 8, NS), F32)] * count,
        ),
        in_specs=[vmem, vmem, hbm] + [anywhere] * (len(operands) - 3),
        out_specs=(anywhere,) * (1 + count),
        scratch_shapes=[
            pltpu.VMEM((count, NZ, NY * FLAT[0], NS), F32),
            pltpu.VMEM((count, NY, NZ, FLAT[1], NS), F32),
            pltpu.VMEM((count, NZ, NY * FLAT[2], NS), F32),
            pltpu.VMEM((4 * SLOTS, 512), BF16),
            pltpu.VMEM((count, 2, SLOTS * 8, NS), F32),
            pltpu.VMEM((count, 2, SLOTS * 8, NS), F32),
            pltpu.SemaphoreType.DMA((count, 7)),
            pltpu.SemaphoreType.DMA((count, 4)),
        ],
        input_output_aliases={} if fresh else {len(operands) - 1: 0},
        compiler_params=pltpu.CompilerParams(vmem_limit_bytes=60 << 20),
        cost_estimate=pl.CostEstimate(flops=count * flops, bytes_accessed=count << 23, transcendentals=0),
    )(*operands)


def place_kernel(steps, *refs):
    count = len(steps)
    blocks, out_ref, sems = refs[:count], refs[-2], refs[-1]
    core, x = lax.axis_index("core"), lax.axis_index("x")
    copies = []
    for n, step in enumerate(steps):
        tile = 4 * before(x, 1 - core, step) + 1 - core
        for q in range(2):
            rows = pl.ds(pl.multiple_of(8 * (tile + 2 * q), 8), 8)
            source = blocks[n].at[q].reshape(SLOTS, 8, NS)
            copies.append(pltpu.make_async_copy(source, out_ref.at[:, rows, :], sems.at[2 * n + q]))
    for copy in copies:
        copy.start()
    for copy in copies:
        copy.wait()


def place(steps, blocks, out):
    anywhere = pl.BlockSpec(memory_space=pl.ANY)
    vmem = pl.BlockSpec(memory_space=pltpu.VMEM)
    count = len(blocks)
    return pl.pallas_call(
        functools.partial(place_kernel, steps),
        out_shape=jax.ShapeDtypeStruct(out.shape, F32),
        in_specs=[vmem] * count + [anywhere],
        out_specs=anywhere,
        scratch_shapes=[pltpu.SemaphoreType.DMA((2 * count,))],
        input_output_aliases={count: 0},
        compiler_params=pltpu.CompilerParams(vmem_limit_bytes=8 << 20),
        cost_estimate=pl.CostEstimate(flops=0, bytes_accessed=count << 21, transcendentals=0),
    )(*blocks, out)


def body(slater, couple_type, couple_multipole, couple_angle, angular, owner_map):
    flat = swap_halves(slater.reshape(COLS * ROWS, NS))
    part_a, part_bc = flat[: FLAT[0]], flat[FLAT[0] :]

    p1, m1, p2, m2 = (shift(part_bc, "z", n) for n in (1, -1, 2, -2))
    a_y = jnp.concatenate([part_a, trade(part_a, "y", 1)], axis=0)
    p1, m1, p2, m2, a_y = together(p1, m1, p2, m2, a_y)
    p3, m3, p4 = shift(p2, "z", 1), shift(m2, "z", -1), shift(p2, "z", 2)
    a_y = jnp.concatenate([a_y, trade(a_y, "y", 2)], axis=0)
    p3, m3, p4, a_y = together(p3, m3, p4, a_y)
    bc = jnp.stack([p3, p2, p1, part_bc, m1, m2, m3, p4])

    b_0, c_0 = bc[:, : FLAT[1]], bc[:, FLAT[1] :]
    b_1, b_3 = turn(b_0, "x", 1), turn(b_0, "x", -1)
    c_1, c_3 = shift(c_0, "y", 1), shift(c_0, "y", -1)
    a_x = jnp.stack([a_y, trade(a_y, "x", 1)])
    b_1, b_3, c_1, c_3, a_x = together(b_1, b_3, c_1, c_3, a_x)
    b_2 = turn(b_1[:4], "x", 1), turn(b_3[4:], "x", -1)
    c_2 = shift(c_1[:4], "y", 1), shift(c_3[4:], "y", -1)
    a_x = jnp.concatenate([a_x, trade(a_x, "x", 2)], axis=0)
    *b_2, c_20, c_21, a_x = together(*b_2, *c_2, a_x)
    b_x = jnp.stack([b_0, b_1, jnp.concatenate(b_2, axis=0), b_3])
    c_y = jnp.concatenate([c_0, c_1, jnp.concatenate([c_20, c_21], axis=0), c_3], axis=1)

    own = mixing(owner_map, couple_type, couple_multipole, couple_angle, angular)

    a_z = lax.all_gather(a_x, "z", axis=0, tiled=False)
    y_1, y_3 = shift(b_x, "y", 1), shift(b_x, "y", -1)
    x_1, x_3 = turn(c_y, "x", 1), turn(c_y, "x", -1)
    other = lax.ppermute(own, "core", [(0, 1), (1, 0)])
    y_1, y_3, x_1, x_3, other = together(y_1, y_3, x_1, x_3, other)
    y_2 = shift(y_1[:2], "y", 1), shift(y_3[2:], "y", -1)
    x_2 = turn(x_1[:4], "x", 1), turn(x_3[4:], "x", -1)

    b_parts, c_parts = [b_x, y_1, *y_2, y_3], [c_y, x_1, *x_2, x_3]
    out, received = None, []
    for steps in ((0, 1, 2), (3,)):
        out, *given = product(steps, own, other, a_z, b_parts, c_parts, out)
        received += [lax.ppermute(block, "core", [(0, 1), (1, 0)]) for block in given]
    out = place((0, 1, 2), received[:3], out)
    return place((3,), received[3:], out)


def solution(mesh):
    fine = Mesh(mesh.devices.reshape(NY, NC, NX, NZ), ("y", "core", "x", "z"))
    groups = ("y", "core")
    return jax.shard_map(
        body,
        mesh=fine,
        in_specs=(
            P(groups, None, ("x", "z"), None),
            P(groups, None),
            P(groups, None),
            P(groups, None),
            P(),
            P(groups),
        ),
        out_specs=P(("y", "core", "x", "z"), None, None),
        check_vma=False,
    )
```

```python
import functools

import jax
import jax.numpy as jnp
from jax import lax
from jax.experimental import pallas as pl
from jax.experimental.pallas import tpu as pltpu
from jax.sharding import Mesh
from jax.sharding import PartitionSpec as P

NY, NC, NX, NZ = 4, 2, 4, 8
ROWS = 4
COLS = 50
CUTS = (10, 20, 20)
FLAT = tuple(ROWS * cut for cut in CUTS)
K = NY * NC * COLS
SLOTS = 128
NS = 128
F32, BF16 = jnp.float32, jnp.bfloat16


def shift(value, axis, step):
    n = lax.axis_size(axis)
    return lax.ppermute(value, axis, [(i, (i + step) % n) for i in range(n)])


def turn(value, axis, step):
    n = lax.axis_size(axis)
    pairs = []
    for c in range(NC):
        for i in range(n):
            j = (i + (step if c == 0 else -step)) % n
            pairs.append((i * NC + c, j * NC + c) if axis == "y" else (c * n + i, c * n + j))
    return lax.ppermute(value, ("y", "core") if axis == "y" else ("core", axis), pairs)


def trade(value, axis, bit):
    n = lax.axis_size(axis)
    return lax.ppermute(value, axis, [(i, i ^ bit) for i in range(n)])


def swap_halves(flat):
    pairs = []
    for c in range(NC):
        for z in range(NZ):
            high = (z >> 1) & 1
            if c == high:
                pairs.append((c * NZ + z, c * NZ + z))
            else:
                pairs.append((c * NZ + z, high * NZ + (z ^ 2)))
    return lax.ppermute(flat, ("core", "z"), pairs)


def together(*values):
    return lax.optimization_barrier(values)


def global_columns(y):
    place = lax.broadcasted_iota(jnp.int32, (K, 1), 0)
    ids, start, offset, first = place, 0, 0, 0
    for part, cut in enumerate(CUTS):
        for half in range(NC):
            for step in range(NY):
                source = y ^ step if part == 0 else lax.rem(y + NY - step, NY)
                now = 100 * source + COLS * half + first - start
                ids = ids + jnp.where(place >= start, now - offset, 0)
                offset, start = now, start + cut
        first += cut
    return ids


def mixing_kernel(owner_ref, kind_ref, pole_ref, angle_ref, angular_ref, out_ref):
    me = lax.axis_index("x") * NZ + lax.axis_index("z")
    pairs = owner_ref.shape[0] * owner_ref.shape[1]
    groups = pairs // 128
    mine = (owner_ref[...] == me).astype(F32)
    low = lax.broadcasted_iota(jnp.int32, (128, 128), 0)
    high = lax.broadcasted_iota(jnp.int32, (128, 128), 1)
    upper = (low <= high).astype(BF16)
    within = jnp.dot(mine.astype(BF16), upper, preferred_element_type=F32)
    totals = jnp.sum(mine, axis=1, keepdims=True)
    before = jnp.zeros((groups, 1), F32)
    row = lax.broadcasted_iota(jnp.int32, (groups, 1), 0)
    for j in range(groups - 1):
        before = before + jnp.where(row > j, totals[j : j + 1, :], 0.0)
    rank = jnp.where(mine > 0.0, within + before - 1.0, -1.0).astype(jnp.int32)
    slot = lax.broadcasted_iota(jnp.int32, (SLOTS, 128), 0)
    chosen = jnp.zeros((24, SLOTS), F32)
    for j in range(groups):
        span = pl.ds(j * 128, 128)
        listed = jnp.concatenate([kind_ref[:, span], pole_ref[:, span], angle_ref[:, span]], axis=0)
        selected = (rank[j : j + 1, :] == slot).astype(BF16)
        chosen = chosen + lax.dot_general(
            listed.astype(F32).astype(BF16),
            selected,
            (((1,), (1,)), ((), ())),
            preferred_element_type=F32,
        )
    count = jnp.sum(totals, axis=0, keepdims=True)
    filled = lax.broadcasted_iota(jnp.int32, (1, SLOTS), 1).astype(F32) < count
    chosen = chosen.astype(jnp.int32)
    column = global_columns(lax.axis_index("y"))
    size = angular_ref.shape[1]
    table = lax.broadcasted_iota(jnp.int32, (size, SLOTS), 0)
    down, across = (lax.broadcasted_iota(jnp.int32, (size, size), d) for d in range(2))
    angular = jnp.sum(jnp.where(down == across, angular_ref[...], 0.0), axis=1, keepdims=True)
    total = jnp.zeros((K, SLOTS), F32)
    for entry in range(8):
        wanted = chosen[entry : entry + 1, :] * 5 + chosen[8 + entry : 9 + entry, :]
        angle = chosen[16 + entry : 17 + entry, :]
        value = jnp.sum(jnp.where(table == angle, angular, 0.0), axis=0, keepdims=True)
        value = jnp.where(filled, value, 0.0)
        total = total + jnp.where(column == wanted, value, 0.0)
    pad = jnp.zeros((512 - K, SLOTS), F32)
    out_ref[...] = jnp.concatenate([total, pad], axis=0).T


def mixing(owner_map, kinds, poles, angles, angular):
    vmem = pl.BlockSpec(memory_space=pltpu.VMEM)
    return pl.pallas_call(
        mixing_kernel,
        out_shape=jax.ShapeDtypeStruct((SLOTS, 512), F32),
        in_specs=[vmem] * 5,
        out_specs=vmem,
        compiler_params=pltpu.CompilerParams(vmem_limit_bytes=16 << 20),
        cost_estimate=pl.CostEstimate(flops=100 << 20, bytes_accessed=1 << 20, transcendentals=0),
    )(owner_map.reshape(-1, 128), kinds.T, poles.T, angles.T, angular[None, :])


def before(x, core, step):
    return lax.rem(x + jnp.where(core == 0, NX - step, step), NX)


def product_kernel(steps, fresh, *refs):
    count = len(steps)
    mix_refs = refs[:2]
    parts = 2 if steps == (2,) else count
    a_ref, b_refs, c_refs = refs[2], refs[3:8], refs[8 : 8 + parts]
    refs = refs[8 + parts + (0 if fresh else 1) :]
    out_ref, send_ref, a_all, b_all, c_all, mix_all, left_all, kept, given, sems, out_sems = refs
    core, x, z = (lax.axis_index(name) for name in ("core", "x", "z"))

    def arrive(n):
        step = steps[n]
        copies = []

        def add(source, target):
            copies.append(pltpu.make_async_copy(source, target, sems.at[n, len(copies)]))

        add(a_ref.at[:, x ^ before(x, core, step)], a_all.at[n])
        add(b_refs[0].at[step], b_all.at[n, 0])
        add(b_refs[1].at[step], b_all.at[n, 1])
        add(b_refs[2 + step // 2].at[step % 2], b_all.at[n, 2])
        add(b_refs[4].at[step], b_all.at[n, 3])
        if step == 2:
            for half in range(2):
                add(c_refs[half], c_all.at[n, pl.ds(4 * half, 4)])
        else:
            add(c_refs[n], c_all.at[n])
        return copies

    def leave(n, q):
        rows = pl.ds(pl.multiple_of(8 * (4 * before(x, core, steps[n]) + core + 2 * q), 8), 8)
        return (
            pltpu.make_async_copy(
                kept.at[n, q].reshape(SLOTS, 8, NS), out_ref.at[:, rows, :], out_sems.at[n, q]
            ),
            pltpu.make_async_copy(given.at[n, q], send_ref.at[n, q], out_sems.at[n, 2 + q]),
        )

    mixes = [
        pltpu.make_async_copy(mix_refs[m], mix_all.at[pl.ds(m * SLOTS, SLOTS)], out_sems.at[0, m]) for m in range(2)
    ]
    for copy in mixes + arrive(0):
        copy.start()
    for copy in mixes:
        copy.wait()
    mix = mix_all[...]
    mix_high = mix.astype(BF16)
    left_all[: 2 * SLOTS, :] = mix_high
    left_all[2 * SLOTS :, :] = (mix - mix_high.astype(F32)).astype(BF16)
    a_run, b_run, c_run = NY * CUTS[0], CUTS[1], NY * CUTS[2]
    pad = jnp.zeros((512 - K, NS), F32)

    for n in range(count):
        for copy in arrive(n):
            copy.wait()
        if n + 1 < count:
            for copy in arrive(n + 1):
                copy.start()

        def one_tile(q, carry, n=n):
            for b in range(2):
                places = [4 * q + 2 * half + b for half in range(2)]
                spots = [lax.rem(place - z + NZ + 3, NZ) for place in places]
                for first in (0, 2):
                    highs, lows = [], []
                    for r in (first, first + 1):
                        pieces = [a_all[n, s, pl.ds(r, a_run, stride=ROWS), :] for s in places]
                        pieces += [
                            b_all[n, y, s, pl.ds(r, b_run, stride=ROWS), :] for s in spots for y in range(NY)
                        ]
                        pieces += [c_all[n, s, pl.ds(r, c_run, stride=ROWS), :] for s in spots]
                        value = jnp.concatenate(pieces + [pad], axis=0)
                        high = value.astype(BF16)
                        highs.append(high)
                        lows.append((value - high.astype(F32)).astype(BF16))
                    right_high = jnp.concatenate(highs, axis=1)
                    right_low = jnp.concatenate(lows, axis=1)
                    full = jnp.dot(left_all[...], right_high, preferred_element_type=F32)
                    rest = jnp.dot(left_all[: 2 * SLOTS, :], right_low, preferred_element_type=F32)
                    total = full[: 2 * SLOTS] + (full[2 * SLOTS :] + rest)
                    for m in range(2):
                        lanes = slice(m * NS, (m + 1) * NS)
                        row = pl.ds(4 * b + first + m, SLOTS, stride=8)
                        kept[n, q, row, :] = total[:SLOTS, lanes]
                        given[n, q, row, :] = total[SLOTS:, lanes]
            for copy in leave(n, q):
                copy.start()
            return carry

        lax.fori_loop(0, 2, one_tile, 0)
    for n in range(count):
        for q in range(2):
            for copy in leave(n, q):
                copy.wait()


def product(steps, own, other, a_part, b_parts, c_parts, out):
    anywhere = pl.BlockSpec(memory_space=pl.ANY)
    fresh, count = out is None, len(steps)
    operands = [own, other, a_part, *b_parts, *c_parts] + ([] if fresh else [out])
    flops = 2 * 8 * 768 * 512 * 256
    return pl.pallas_call(
        functools.partial(product_kernel, steps, fresh),
        out_shape=(
            jax.ShapeDtypeStruct((SLOTS, NS, NS), F32),
            jax.ShapeDtypeStruct((count, 2, SLOTS * 8, NS), F32),
        ),
        in_specs=[anywhere] * len(operands),
        out_specs=(anywhere, anywhere),
        scratch_shapes=[
            pltpu.VMEM((count, NZ, NY * FLAT[0], NS), F32),
            pltpu.VMEM((count, NY, NZ, FLAT[1], NS), F32),
            pltpu.VMEM((count, NZ, NY * FLAT[2], NS), F32),
            pltpu.VMEM((2 * SLOTS, 512), F32),
            pltpu.VMEM((4 * SLOTS, 512), BF16),
            pltpu.VMEM((count, 2, SLOTS * 8, NS), F32),
            pltpu.VMEM((count, 2, SLOTS * 8, NS), F32),
            pltpu.SemaphoreType.DMA((count, 7)),
            pltpu.SemaphoreType.DMA((count, 4)),
        ],
        input_output_aliases={} if fresh else {len(operands) - 1: 0},
        compiler_params=pltpu.CompilerParams(vmem_limit_bytes=60 << 20),
        cost_estimate=pl.CostEstimate(flops=count * flops, bytes_accessed=count << 23, transcendentals=0),
    )(*operands)


def place_kernel(steps, blocks_ref, _, out_ref, sems):
    core, x = lax.axis_index("core"), lax.axis_index("x")
    copies = []
    for n, step in enumerate(steps):
        tile = 4 * before(x, 1 - core, step) + 1 - core
        for q in range(2):
            rows = pl.ds(pl.multiple_of(8 * (tile + 2 * q), 8), 8)
            source = blocks_ref.at[n, q].reshape(SLOTS, 8, NS)
            copies.append(pltpu.make_async_copy(source, out_ref.at[:, rows, :], sems.at[n, q]))
    for copy in copies:
        copy.start()
    for copy in copies:
        copy.wait()


def place(steps, blocks, out):
    anywhere = pl.BlockSpec(memory_space=pl.ANY)
    vmem = pl.BlockSpec(memory_space=pltpu.VMEM)
    count = len(steps)
    return pl.pallas_call(
        functools.partial(place_kernel, steps),
        out_shape=jax.ShapeDtypeStruct(out.shape, F32),
        in_specs=[vmem, anywhere],
        out_specs=anywhere,
        scratch_shapes=[pltpu.SemaphoreType.DMA((count, 2))],
        input_output_aliases={1: 0},
        compiler_params=pltpu.CompilerParams(vmem_limit_bytes=8 << 20),
        cost_estimate=pl.CostEstimate(flops=0, bytes_accessed=count << 21, transcendentals=0),
    )(blocks, out)


def body(slater, couple_type, couple_multipole, couple_angle, angular, owner_map):
    flat = swap_halves(slater.reshape(COLS * ROWS, NS))
    part_a, part_bc = flat[: FLAT[0]], flat[FLAT[0] :]

    p1, m1, p2, m2 = (shift(part_bc, "z", n) for n in (1, -1, 2, -2))
    a_y = jnp.concatenate([part_a, trade(part_a, "y", 1)], axis=0)
    p1, m1, p2, m2, a_y = together(p1, m1, p2, m2, a_y)
    p3, m3, p4 = shift(p2, "z", 1), shift(m2, "z", -1), shift(p2, "z", 2)
    a_y = jnp.concatenate([a_y, trade(a_y, "y", 2)], axis=0)
    p3, m3, p4, a_y = together(p3, m3, p4, a_y)
    bc = jnp.stack([p3, p2, p1, part_bc, m1, m2, m3, p4])

    b_0, c_0 = bc[:, : FLAT[1]], bc[:, FLAT[1] :]
    b_1, b_3 = turn(b_0, "x", 1), turn(b_0, "x", -1)
    c_1, c_3 = shift(c_0, "y", 1), shift(c_0, "y", -1)
    a_x = jnp.stack([a_y, trade(a_y, "x", 1)])
    b_1, b_3, c_1, c_3, a_x = together(b_1, b_3, c_1, c_3, a_x)
    b_2 = turn(b_1[:4], "x", 1), turn(b_3[4:], "x", -1)
    c_2 = shift(c_1[:4], "y", 1), shift(c_3[4:], "y", -1)
    a_x = jnp.concatenate([a_x, trade(a_x, "x", 2)], axis=0)
    *b_2, c_20, c_21, a_x = together(*b_2, *c_2, a_x)
    b_x = jnp.stack([b_0, b_1, jnp.concatenate(b_2, axis=0), b_3])
    c_y = jnp.concatenate([c_0, c_1, jnp.concatenate([c_20, c_21], axis=0), c_3], axis=1)

    own = mixing(owner_map, couple_type, couple_multipole, couple_angle, angular)

    a_z = lax.all_gather(a_x, "z", axis=0, tiled=False)
    y_1, y_3 = shift(b_x, "y", 1), shift(b_x, "y", -1)
    x_1, x_3 = turn(c_y, "x", 1), turn(c_y, "x", -1)
    other = lax.ppermute(own, "core", [(0, 1), (1, 0)])
    y_1, y_3, x_1, x_3, other = together(y_1, y_3, x_1, x_3, other)
    y_2 = shift(y_1[:2], "y", 1), shift(y_3[2:], "y", -1)
    x_2 = turn(x_1[:4], "x", 1), turn(x_3[4:], "x", -1)
    *y_2, x_20, x_21 = together(*y_2, *x_2)
    x_2 = x_20, x_21

    b_parts = [b_x, y_1, *y_2, y_3]
    out = None
    received = []
    for steps, c_parts in (((0, 1, 3), (c_y, x_1, x_3)), ((2,), x_2)):
        out, given = product(steps, own, other, a_z, b_parts, c_parts, out)
        received.append(lax.ppermute(given, "core", [(0, 1), (1, 0)]))
    out = place((0, 1, 3), received[0], out)
    return place((2,), received[1], out)


def solution(mesh):
    fine = Mesh(mesh.devices.reshape(NY, NC, NX, NZ), ("y", "core", "x", "z"))
    groups = ("y", "core")
    return jax.shard_map(
        body,
        mesh=fine,
        in_specs=(
            P(groups, None, ("x", "z"), None),
            P(groups, None),
            P(groups, None),
            P(groups, None),
            P(),
            P(groups),
        ),
        out_specs=P(("y", "core", "x", "z"), None, None),
        check_vma=False,
    )
```

```python
import functools

import jax
import jax.numpy as jnp
from jax import lax
from jax.experimental import pallas as pl
from jax.experimental.pallas import tpu as pltpu
from jax.sharding import Mesh
from jax.sharding import PartitionSpec as P

NY, NC, NX, NZ = 4, 2, 4, 8
ROWS = 4
COLS = 50
CUTS = (10, 20, 20)
FLAT = tuple(ROWS * cut for cut in CUTS)
K = NY * NC * COLS
SLOTS = 128
NS = 128
F32, BF16 = jnp.float32, jnp.bfloat16


def shift(value, axis, step):
    n = lax.axis_size(axis)
    return lax.ppermute(value, axis, [(i, (i + step) % n) for i in range(n)])


def turn(value, axis, step):
    n = lax.axis_size(axis)
    pairs = []
    for c in range(NC):
        for i in range(n):
            j = (i + (step if c == 0 else -step)) % n
            pairs.append((i * NC + c, j * NC + c) if axis == "y" else (c * n + i, c * n + j))
    return lax.ppermute(value, ("y", "core") if axis == "y" else ("core", axis), pairs)


def trade(value, axis, bit):
    n = lax.axis_size(axis)
    return lax.ppermute(value, axis, [(i, i ^ bit) for i in range(n)])


def swap_halves(flat):
    pairs = []
    for c in range(NC):
        for z in range(NZ):
            high = (z >> 1) & 1
            if c == high:
                pairs.append((c * NZ + z, c * NZ + z))
            else:
                pairs.append((c * NZ + z, high * NZ + (z ^ 2)))
    return lax.ppermute(flat, ("core", "z"), pairs)


def together(*values):
    return lax.optimization_barrier(values)


def global_columns(y):
    place = lax.broadcasted_iota(jnp.int32, (K, 1), 0)
    ids, start, offset, first = place, 0, 0, 0
    for part, cut in enumerate(CUTS):
        for half in range(NC):
            for step in range(NY):
                source = y ^ step if part == 0 else lax.rem(y + NY - step, NY)
                now = 100 * source + COLS * half + first - start
                ids = ids + jnp.where(place >= start, now - offset, 0)
                offset, start = now, start + cut
        first += cut
    return ids


def mixing_kernel(owner_ref, kind_ref, pole_ref, angle_ref, angular_ref, out_ref):
    me = lax.axis_index("x") * NZ + lax.axis_index("z")
    pairs = owner_ref.shape[0] * owner_ref.shape[1]
    groups = pairs // 128
    mine = (owner_ref[...] == me).astype(F32)
    low = lax.broadcasted_iota(jnp.int32, (128, 128), 0)
    high = lax.broadcasted_iota(jnp.int32, (128, 128), 1)
    upper = (low <= high).astype(BF16)
    within = jnp.dot(mine.astype(BF16), upper, preferred_element_type=F32)
    totals = jnp.sum(mine, axis=1, keepdims=True)
    before = jnp.zeros((groups, 1), F32)
    row = lax.broadcasted_iota(jnp.int32, (groups, 1), 0)
    for j in range(groups - 1):
        before = before + jnp.where(row > j, totals[j : j + 1, :], 0.0)
    rank = jnp.where(mine > 0.0, within + before - 1.0, -1.0).astype(jnp.int32)
    slot = lax.broadcasted_iota(jnp.int32, (SLOTS, 128), 0)
    chosen = jnp.zeros((24, SLOTS), F32)
    for j in range(groups):
        span = pl.ds(j * 128, 128)
        listed = jnp.concatenate([kind_ref[:, span], pole_ref[:, span], angle_ref[:, span]], axis=0)
        selected = (rank[j : j + 1, :] == slot).astype(BF16)
        chosen = chosen + lax.dot_general(
            listed.astype(F32).astype(BF16),
            selected,
            (((1,), (1,)), ((), ())),
            preferred_element_type=F32,
        )
    count = jnp.sum(totals, axis=0, keepdims=True)
    filled = lax.broadcasted_iota(jnp.int32, (1, SLOTS), 1).astype(F32) < count
    chosen = chosen.astype(jnp.int32)
    column = global_columns(lax.axis_index("y"))
    size = angular_ref.shape[1]
    table = lax.broadcasted_iota(jnp.int32, (size, SLOTS), 0)
    down, across = (lax.broadcasted_iota(jnp.int32, (size, size), d) for d in range(2))
    angular = jnp.sum(jnp.where(down == across, angular_ref[...], 0.0), axis=1, keepdims=True)
    total = jnp.zeros((K, SLOTS), F32)
    for entry in range(8):
        wanted = chosen[entry : entry + 1, :] * 5 + chosen[8 + entry : 9 + entry, :]
        angle = chosen[16 + entry : 17 + entry, :]
        value = jnp.sum(jnp.where(table == angle, angular, 0.0), axis=0, keepdims=True)
        value = jnp.where(filled, value, 0.0)
        total = total + jnp.where(column == wanted, value, 0.0)
    pad = jnp.zeros((512 - K, SLOTS), F32)
    out_ref[...] = jnp.concatenate([total, pad], axis=0).T


def mixing(owner_map, kinds, poles, angles, angular):
    vmem = pl.BlockSpec(memory_space=pltpu.VMEM)
    return pl.pallas_call(
        mixing_kernel,
        out_shape=jax.ShapeDtypeStruct((SLOTS, 512), F32),
        in_specs=[vmem] * 5,
        out_specs=vmem,
        compiler_params=pltpu.CompilerParams(vmem_limit_bytes=16 << 20),
        cost_estimate=pl.CostEstimate(flops=100 << 20, bytes_accessed=1 << 20, transcendentals=0),
    )(owner_map.reshape(-1, 128), kinds.T, poles.T, angles.T, angular[None, :])


def before(x, core, step):
    return lax.rem(x + jnp.where(core == 0, NX - step, step), NX)


def product_kernel(steps, fresh, *refs):
    count = len(steps)
    mix_refs = refs[:2]
    parts = 2 if steps == (2,) else count
    a_ref, b_refs, c_refs = refs[2], refs[3:8], refs[8 : 8 + parts]
    refs = refs[8 + parts + (0 if fresh else 1) :]
    out_ref, send_ref, a_all, b_all, c_all, mix_all, left_all, kept, given, sems, out_sems = refs
    core, x, z = (lax.axis_index(name) for name in ("core", "x", "z"))

    def arrive(n):
        step = steps[n]
        copies = []

        def add(source, target):
            copies.append(pltpu.make_async_copy(source, target, sems.at[n, len(copies)]))

        add(a_ref.at[:, x ^ before(x, core, step)], a_all.at[n])
        add(b_refs[0].at[step], b_all.at[n, 0])
        add(b_refs[1].at[step], b_all.at[n, 1])
        add(b_refs[2 + step // 2].at[step % 2], b_all.at[n, 2])
        add(b_refs[4].at[step], b_all.at[n, 3])
        if step == 2:
            for half in range(2):
                add(c_refs[half], c_all.at[n, pl.ds(4 * half, 4)])
        else:
            add(c_refs[n], c_all.at[n])
        return copies

    def leave(n, q):
        rows = pl.ds(pl.multiple_of(8 * (4 * before(x, core, steps[n]) + core + 2 * q), 8), 8)
        return (
            pltpu.make_async_copy(
                kept.at[n, q].reshape(SLOTS, 8, NS), out_ref.at[:, rows, :], out_sems.at[n, q]
            ),
            pltpu.make_async_copy(given.at[n, q], send_ref.at[n, q], out_sems.at[n, 2 + q]),
        )

    mixes = [
        pltpu.make_async_copy(mix_refs[m], mix_all.at[pl.ds(m * SLOTS, SLOTS)], out_sems.at[0, m]) for m in range(2)
    ]
    for copy in mixes + arrive(0):
        copy.start()
    for copy in mixes:
        copy.wait()
    mix = mix_all[...]
    mix_high = mix.astype(BF16)
    left_all[: 2 * SLOTS, :] = mix_high
    left_all[2 * SLOTS :, :] = (mix - mix_high.astype(F32)).astype(BF16)
    a_run, b_run, c_run = NY * CUTS[0], CUTS[1], NY * CUTS[2]
    pad = jnp.zeros((512 - K, NS), F32)

    for n in range(count):
        for copy in arrive(n):
            copy.wait()
        if n + 1 < count:
            for copy in arrive(n + 1):
                copy.start()

        def one_tile(q, carry, n=n):
            for b in range(2):
                places = [4 * q + 2 * half + b for half in range(2)]
                spots = [lax.rem(place - z + NZ + 3, NZ) for place in places]
                for first in (0, 2):
                    highs, lows = [], []
                    for r in (first, first + 1):
                        pieces = [a_all[n, s, pl.ds(r, a_run, stride=ROWS), :] for s in places]
                        pieces += [
                            b_all[n, y, s, pl.ds(r, b_run, stride=ROWS), :] for s in spots for y in range(NY)
                        ]
                        pieces += [c_all[n, s, pl.ds(r, c_run, stride=ROWS), :] for s in spots]
                        value = jnp.concatenate(pieces + [pad], axis=0)
                        high = value.astype(BF16)
                        highs.append(high)
                        lows.append((value - high.astype(F32)).astype(BF16))
                    right_high = jnp.concatenate(highs, axis=1)
                    right_low = jnp.concatenate(lows, axis=1)
                    full = jnp.dot(left_all[...], right_high, preferred_element_type=F32)
                    rest = jnp.dot(left_all[: 2 * SLOTS, :], right_low, preferred_element_type=F32)
                    total = full[: 2 * SLOTS] + (full[2 * SLOTS :] + rest)
                    for m in range(2):
                        lanes = slice(m * NS, (m + 1) * NS)
                        row = pl.ds(4 * b + first + m, SLOTS, stride=8)
                        kept[n, q, row, :] = total[:SLOTS, lanes]
                        given[n, q, row, :] = total[SLOTS:, lanes]
            for copy in leave(n, q):
                copy.start()
            return carry

        lax.fori_loop(0, 2, one_tile, 0)
    for n in range(count):
        for q in range(2):
            for copy in leave(n, q):
                copy.wait()


def product(steps, own, other, a_part, b_parts, c_parts, out):
    anywhere = pl.BlockSpec(memory_space=pl.ANY)
    fresh, count = out is None, len(steps)
    operands = [own, other, a_part, *b_parts, *c_parts] + ([] if fresh else [out])
    flops = 2 * 8 * 768 * 512 * 256
    return pl.pallas_call(
        functools.partial(product_kernel, steps, fresh),
        out_shape=(
            jax.ShapeDtypeStruct((SLOTS, NS, NS), F32),
            jax.ShapeDtypeStruct((count, 2, SLOTS * 8, NS), F32),
        ),
        in_specs=[anywhere] * len(operands),
        out_specs=(anywhere, anywhere),
        scratch_shapes=[
            pltpu.VMEM((count, NZ, NY * FLAT[0], NS), F32),
            pltpu.VMEM((count + 1, NY, NZ, FLAT[1], NS), F32),
            pltpu.VMEM((count, NZ, NY * FLAT[2], NS), F32),
            pltpu.VMEM((2 * SLOTS, 512), F32),
            pltpu.VMEM((4 * SLOTS, 512), BF16),
            pltpu.VMEM((count, 2, SLOTS * 8, NS), F32),
            pltpu.VMEM((count, 2, SLOTS * 8, NS), F32),
            pltpu.SemaphoreType.DMA((count, 7)),
            pltpu.SemaphoreType.DMA((count, 4)),
        ],
        input_output_aliases={} if fresh else {len(operands) - 1: 0},
        compiler_params=pltpu.CompilerParams(vmem_limit_bytes=60 << 20),
        cost_estimate=pl.CostEstimate(flops=count * flops, bytes_accessed=count << 23, transcendentals=0),
    )(*operands)


def place_kernel(steps, blocks_ref, _, out_ref, sems):
    core, x = lax.axis_index("core"), lax.axis_index("x")
    copies = []
    for n, step in enumerate(steps):
        tile = 4 * before(x, 1 - core, step) + 1 - core
        for q in range(2):
            rows = pl.ds(pl.multiple_of(8 * (tile + 2 * q), 8), 8)
            source = blocks_ref.at[n, q].reshape(SLOTS, 8, NS)
            copies.append(pltpu.make_async_copy(source, out_ref.at[:, rows, :], sems.at[n, q]))
    for copy in copies:
        copy.start()
    for copy in copies:
        copy.wait()


def place(steps, blocks, out):
    anywhere = pl.BlockSpec(memory_space=pl.ANY)
    vmem = pl.BlockSpec(memory_space=pltpu.VMEM)
    count = len(steps)
    return pl.pallas_call(
        functools.partial(place_kernel, steps),
        out_shape=jax.ShapeDtypeStruct(out.shape, F32),
        in_specs=[vmem, anywhere],
        out_specs=anywhere,
        scratch_shapes=[pltpu.SemaphoreType.DMA((count, 2))],
        input_output_aliases={1: 0},
        compiler_params=pltpu.CompilerParams(vmem_limit_bytes=8 << 20),
        cost_estimate=pl.CostEstimate(flops=0, bytes_accessed=count << 21, transcendentals=0),
    )(blocks, out)


def body(slater, couple_type, couple_multipole, couple_angle, angular, owner_map):
    flat = swap_halves(slater.reshape(COLS * ROWS, NS))
    part_a, part_bc = flat[: FLAT[0]], flat[FLAT[0] :]

    p1, m1, p2, m2 = (shift(part_bc, "z", n) for n in (1, -1, 2, -2))
    a_y = jnp.concatenate([part_a, trade(part_a, "y", 1)], axis=0)
    p1, m1, p2, m2, a_y = together(p1, m1, p2, m2, a_y)
    p3, m3, p4 = shift(p2, "z", 1), shift(m2, "z", -1), shift(p2, "z", 2)
    a_y = jnp.concatenate([a_y, trade(a_y, "y", 2)], axis=0)
    p3, m3, p4, a_y = together(p3, m3, p4, a_y)
    bc = jnp.stack([p3, p2, p1, part_bc, m1, m2, m3, p4])

    b_0, c_0 = bc[:, : FLAT[1]], bc[:, FLAT[1] :]
    b_1, b_3 = turn(b_0, "x", 1), turn(b_0, "x", -1)
    c_1, c_3 = shift(c_0, "y", 1), shift(c_0, "y", -1)
    a_x = jnp.stack([a_y, trade(a_y, "x", 1)])
    b_1, b_3, c_1, c_3, a_x = together(b_1, b_3, c_1, c_3, a_x)
    b_2 = turn(b_1[:4], "x", 1), turn(b_3[4:], "x", -1)
    c_2 = shift(c_1[:4], "y", 1), shift(c_3[4:], "y", -1)
    a_x = jnp.concatenate([a_x, trade(a_x, "x", 2)], axis=0)
    *b_2, c_20, c_21, a_x = together(*b_2, *c_2, a_x)
    b_x = jnp.stack([b_0, b_1, jnp.concatenate(b_2, axis=0), b_3])
    c_y = jnp.concatenate([c_0, c_1, jnp.concatenate([c_20, c_21], axis=0), c_3], axis=1)

    own = mixing(owner_map, couple_type, couple_multipole, couple_angle, angular)

    a_z = lax.all_gather(a_x, "z", axis=0, tiled=False)
    y_1, y_3 = shift(b_x, "y", 1), shift(b_x, "y", -1)
    x_1, x_3 = turn(c_y, "x", 1), turn(c_y, "x", -1)
    other = lax.ppermute(own, "core", [(0, 1), (1, 0)])
    y_1, y_3, x_1, x_3, other = together(y_1, y_3, x_1, x_3, other)
    y_2 = shift(y_1[:2], "y", 1), shift(y_3[2:], "y", -1)
    x_2 = turn(x_1[:4], "x", 1), turn(x_3[4:], "x", -1)
    *y_2, x_20, x_21 = together(*y_2, *x_2)
    x_2 = x_20, x_21

    b_parts = [b_x, y_1, *y_2, y_3]
    out = None
    received = []
    for steps, c_parts in (((0, 1, 3), (c_y, x_1, x_3)), ((2,), x_2)):
        out, given = product(steps, own, other, a_z, b_parts, c_parts, out)
        received.append(lax.ppermute(given, "core", [(0, 1), (1, 0)]))
    out = place((0, 1, 3), received[0], out)
    return place((2,), received[1], out)


def solution(mesh):
    fine = Mesh(mesh.devices.reshape(NY, NC, NX, NZ), ("y", "core", "x", "z"))
    groups = ("y", "core")
    return jax.shard_map(
        body,
        mesh=fine,
        in_specs=(
            P(groups, None, ("x", "z"), None),
            P(groups, None),
            P(groups, None),
            P(groups, None),
            P(),
            P(groups),
        ),
        out_specs=P(("y", "core", "x", "z"), None, None),
        check_vma=False,
    )
```

```python
import functools

import jax
import jax.numpy as jnp
from jax import lax
from jax.experimental import pallas as pl
from jax.experimental.pallas import tpu as pltpu
from jax.sharding import Mesh
from jax.sharding import PartitionSpec as P

NY, NC, NX, NZ = 4, 2, 4, 8
ROWS = 4
COLS = 50
CUTS = (10, 20, 20)
FLAT = tuple(ROWS * cut for cut in CUTS)
K = NY * NC * COLS
SLOTS = 128
NS = 128
F32, BF16 = jnp.float32, jnp.bfloat16


def shift(value, axis, step):
    n = lax.axis_size(axis)
    return lax.ppermute(value, axis, [(i, (i + step) % n) for i in range(n)])


def turn(value, axis, step):
    n = lax.axis_size(axis)
    pairs = []
    for c in range(NC):
        for i in range(n):
            j = (i + (step if c == 0 else -step)) % n
            pairs.append((i * NC + c, j * NC + c) if axis == "y" else (c * n + i, c * n + j))
    return lax.ppermute(value, ("y", "core") if axis == "y" else ("core", axis), pairs)


def trade(value, axis, bit):
    n = lax.axis_size(axis)
    return lax.ppermute(value, axis, [(i, i ^ bit) for i in range(n)])


def swap_halves(flat):
    pairs = []
    for c in range(NC):
        for z in range(NZ):
            high = (z >> 1) & 1
            if c == high:
                pairs.append((c * NZ + z, c * NZ + z))
            else:
                pairs.append((c * NZ + z, high * NZ + (z ^ 2)))
    return lax.ppermute(flat, ("core", "z"), pairs)


def together(*values):
    return lax.optimization_barrier(values)


def global_columns(y):
    place = lax.broadcasted_iota(jnp.int32, (K, 1), 0)
    ids, start, offset, first = place, 0, 0, 0
    for part, cut in enumerate(CUTS):
        for half in range(NC):
            for step in range(NY):
                source = y ^ step if part == 0 else lax.rem(y + NY - step, NY)
                now = 100 * source + COLS * half + first - start
                ids = ids + jnp.where(place >= start, now - offset, 0)
                offset, start = now, start + cut
        first += cut
    return ids


def mixing_kernel(owner_ref, kind_ref, pole_ref, angle_ref, angular_ref, out_ref):
    me = lax.axis_index("x") * NZ + lax.axis_index("z")
    pairs = owner_ref.shape[0] * owner_ref.shape[1]
    groups = pairs // 128
    mine = (owner_ref[...] == me).astype(F32)
    low = lax.broadcasted_iota(jnp.int32, (128, 128), 0)
    high = lax.broadcasted_iota(jnp.int32, (128, 128), 1)
    upper = (low <= high).astype(BF16)
    within = jnp.dot(mine.astype(BF16), upper, preferred_element_type=F32)
    totals = jnp.sum(mine, axis=1, keepdims=True)
    before = jnp.zeros((groups, 1), F32)
    row = lax.broadcasted_iota(jnp.int32, (groups, 1), 0)
    for j in range(groups - 1):
        before = before + jnp.where(row > j, totals[j : j + 1, :], 0.0)
    rank = jnp.where(mine > 0.0, within + before - 1.0, -1.0).astype(jnp.int32)
    slot = lax.broadcasted_iota(jnp.int32, (SLOTS, 128), 0)
    chosen = jnp.zeros((24, SLOTS), F32)
    for j in range(groups):
        span = pl.ds(j * 128, 128)
        listed = jnp.concatenate([kind_ref[:, span], pole_ref[:, span], angle_ref[:, span]], axis=0)
        selected = (rank[j : j + 1, :] == slot).astype(BF16)
        chosen = chosen + lax.dot_general(
            listed.astype(F32).astype(BF16),
            selected,
            (((1,), (1,)), ((), ())),
            preferred_element_type=F32,
        )
    count = jnp.sum(totals, axis=0, keepdims=True)
    filled = lax.broadcasted_iota(jnp.int32, (1, SLOTS), 1).astype(F32) < count
    chosen = chosen.astype(jnp.int32)
    column = global_columns(lax.axis_index("y"))
    size = angular_ref.shape[1]
    table = lax.broadcasted_iota(jnp.int32, (size, SLOTS), 0)
    down, across = (lax.broadcasted_iota(jnp.int32, (size, size), d) for d in range(2))
    angular = jnp.sum(jnp.where(down == across, angular_ref[...], 0.0), axis=1, keepdims=True)
    total = jnp.zeros((K, SLOTS), F32)
    for entry in range(8):
        wanted = chosen[entry : entry + 1, :] * 5 + chosen[8 + entry : 9 + entry, :]
        angle = chosen[16 + entry : 17 + entry, :]
        value = jnp.sum(jnp.where(table == angle, angular, 0.0), axis=0, keepdims=True)
        value = jnp.where(filled, value, 0.0)
        total = total + jnp.where(column == wanted, value, 0.0)
    pad = jnp.zeros((512 - K, SLOTS), F32)
    out_ref[...] = jnp.concatenate([total, pad], axis=0).T


def mixing(owner_map, kinds, poles, angles, angular):
    vmem = pl.BlockSpec(memory_space=pltpu.VMEM)
    return pl.pallas_call(
        mixing_kernel,
        out_shape=jax.ShapeDtypeStruct((SLOTS, 512), F32),
        in_specs=[vmem] * 5,
        out_specs=vmem,
        compiler_params=pltpu.CompilerParams(vmem_limit_bytes=16 << 20),
        cost_estimate=pl.CostEstimate(flops=100 << 20, bytes_accessed=1 << 20, transcendentals=0),
    )(owner_map.reshape(-1, 128), kinds.T, poles.T, angles.T, angular[None, :])


def before(x, core, step):
    return lax.rem(x + jnp.where(core == 0, NX - step, step), NX)


def product_kernel(steps, fresh, *refs):
    count = len(steps)
    mix_refs = refs[:2]
    parts = 2 if steps == (2,) else count
    a_ref, b_refs, c_refs = refs[2], refs[3:8], refs[8 : 8 + parts]
    refs = refs[8 + parts + (0 if fresh else 1) :]
    out_ref, send_ref, a_all, b_all, c_all, mix_all, left_all, kept, given, sems, out_sems = refs
    core, x, z = (lax.axis_index(name) for name in ("core", "x", "z"))

    def arrive(n):
        step = steps[n]
        copies = []

        def add(source, target):
            copies.append(pltpu.make_async_copy(source, target, sems.at[n, len(copies)]))

        add(a_ref.at[:, x ^ before(x, core, step)], a_all.at[n])
        add(b_refs[0].at[step], b_all.at[n, 0])
        add(b_refs[1].at[step], b_all.at[n, 1])
        add(b_refs[2 + step // 2].at[step % 2], b_all.at[n, 2])
        add(b_refs[4].at[step], b_all.at[n, 3])
        if step == 2:
            for half in range(2):
                add(c_refs[half], c_all.at[n, pl.ds(4 * half, 4)])
        else:
            add(c_refs[n], c_all.at[n])
        return copies

    def leave(n, q):
        rows = pl.ds(pl.multiple_of(8 * (4 * before(x, core, steps[n]) + core + 2 * q), 8), 8)
        return (
            pltpu.make_async_copy(
                kept.at[n, q].reshape(SLOTS, 8, NS), out_ref.at[:, rows, :], out_sems.at[n, q]
            ),
            pltpu.make_async_copy(given.at[n, q], send_ref.at[n, q], out_sems.at[n, 2 + q]),
        )

    mixes = [
        pltpu.make_async_copy(mix_refs[m], mix_all.at[pl.ds(m * SLOTS, SLOTS)], out_sems.at[0, m]) for m in range(2)
    ]
    for copy in mixes + arrive(0):
        copy.start()
    for copy in mixes:
        copy.wait()
    mix = mix_all[...]
    mix_high = mix.astype(BF16)
    mix_low = (mix - mix_high.astype(F32)).astype(BF16)
    tail = jnp.zeros((2 * SLOTS, 1280 - 3 * K), BF16)
    left_all[...] = jnp.concatenate([mix_high[:, :K], mix_low[:, :K], mix_high[:, :K], tail], axis=1)
    a_run, b_run, c_run = NY * CUTS[0], CUTS[1], NY * CUTS[2]
    pad = jnp.zeros((1280 - 3 * K, 2 * NS), BF16)

    for n in range(count):
        for copy in arrive(n):
            copy.wait()
        if n + 1 < count:
            for copy in arrive(n + 1):
                copy.start()

        def one_tile(q, carry, n=n):
            for b in range(2):
                places = [4 * q + 2 * half + b for half in range(2)]
                spots = [lax.rem(place - z + NZ + 3, NZ) for place in places]
                for first in (0, 2):
                    highs, lows = [], []
                    for r in (first, first + 1):
                        pieces = [a_all[n, s, pl.ds(r, a_run, stride=ROWS), :] for s in places]
                        pieces += [
                            b_all[n, y, s, pl.ds(r, b_run, stride=ROWS), :] for s in spots for y in range(NY)
                        ]
                        pieces += [c_all[n, s, pl.ds(r, c_run, stride=ROWS), :] for s in spots]
                        value = jnp.concatenate(pieces, axis=0)
                        high = value.astype(BF16)
                        highs.append(high)
                        lows.append((value - high.astype(F32)).astype(BF16))
                    right_high = jnp.concatenate(highs, axis=1)
                    right_low = jnp.concatenate(lows, axis=1)
                    right = jnp.concatenate([right_high, right_high, right_low, pad], axis=0)
                    total = jnp.dot(left_all[...], right, preferred_element_type=F32)
                    for m in range(2):
                        lanes = slice(m * NS, (m + 1) * NS)
                        row = pl.ds(4 * b + first + m, SLOTS, stride=8)
                        kept[n, q, row, :] = total[:SLOTS, lanes]
                        given[n, q, row, :] = total[SLOTS:, lanes]
            for copy in leave(n, q):
                copy.start()
            return carry

        lax.fori_loop(0, 2, one_tile, 0)
    for n in range(count):
        for q in range(2):
            for copy in leave(n, q):
                copy.wait()


def product(steps, own, other, a_part, b_parts, c_parts, out):
    anywhere = pl.BlockSpec(memory_space=pl.ANY)
    fresh, count = out is None, len(steps)
    operands = [own, other, a_part, *b_parts, *c_parts] + ([] if fresh else [out])
    flops = 2 * 8 * 768 * 512 * 256
    return pl.pallas_call(
        functools.partial(product_kernel, steps, fresh),
        out_shape=(
            jax.ShapeDtypeStruct((SLOTS, NS, NS), F32),
            jax.ShapeDtypeStruct((count, 2, SLOTS * 8, NS), F32),
        ),
        in_specs=[anywhere] * len(operands),
        out_specs=(anywhere, anywhere),
        scratch_shapes=[
            pltpu.VMEM((count, NZ, NY * FLAT[0], NS), F32),
            pltpu.VMEM((count + 1, NY, NZ, FLAT[1], NS), F32),
            pltpu.VMEM((count, NZ, NY * FLAT[2], NS), F32),
            pltpu.VMEM((2 * SLOTS, 512), F32),
            pltpu.VMEM((2 * SLOTS, 1280), BF16),
            pltpu.VMEM((count, 2, SLOTS * 8, NS), F32),
            pltpu.VMEM((count, 2, SLOTS * 8, NS), F32),
            pltpu.SemaphoreType.DMA((count, 7)),
            pltpu.SemaphoreType.DMA((count, 4)),
        ],
        input_output_aliases={} if fresh else {len(operands) - 1: 0},
        compiler_params=pltpu.CompilerParams(vmem_limit_bytes=60 << 20),
        cost_estimate=pl.CostEstimate(flops=count * flops, bytes_accessed=count << 23, transcendentals=0),
    )(*operands)


def place_kernel(steps, blocks_ref, _, out_ref, sems):
    core, x = lax.axis_index("core"), lax.axis_index("x")
    copies = []
    for n, step in enumerate(steps):
        tile = 4 * before(x, 1 - core, step) + 1 - core
        for q in range(2):
            rows = pl.ds(pl.multiple_of(8 * (tile + 2 * q), 8), 8)
            source = blocks_ref.at[n, q].reshape(SLOTS, 8, NS)
            copies.append(pltpu.make_async_copy(source, out_ref.at[:, rows, :], sems.at[n, q]))
    for copy in copies:
        copy.start()
    for copy in copies:
        copy.wait()


def place(steps, blocks, out):
    anywhere = pl.BlockSpec(memory_space=pl.ANY)
    vmem = pl.BlockSpec(memory_space=pltpu.VMEM)
    count = len(steps)
    return pl.pallas_call(
        functools.partial(place_kernel, steps),
        out_shape=jax.ShapeDtypeStruct(out.shape, F32),
        in_specs=[vmem, anywhere],
        out_specs=anywhere,
        scratch_shapes=[pltpu.SemaphoreType.DMA((count, 2))],
        input_output_aliases={1: 0},
        compiler_params=pltpu.CompilerParams(vmem_limit_bytes=8 << 20),
        cost_estimate=pl.CostEstimate(flops=0, bytes_accessed=count << 21, transcendentals=0),
    )(blocks, out)


def body(slater, couple_type, couple_multipole, couple_angle, angular, owner_map):
    flat = swap_halves(slater.reshape(COLS * ROWS, NS))
    part_a, part_bc = flat[: FLAT[0]], flat[FLAT[0] :]

    p1, m1, p2, m2 = (shift(part_bc, "z", n) for n in (1, -1, 2, -2))
    a_y = jnp.concatenate([part_a, trade(part_a, "y", 1)], axis=0)
    p1, m1, p2, m2, a_y = together(p1, m1, p2, m2, a_y)
    p3, m3, p4 = shift(p2, "z", 1), shift(m2, "z", -1), shift(p2, "z", 2)
    a_y = jnp.concatenate([a_y, trade(a_y, "y", 2)], axis=0)
    p3, m3, p4, a_y = together(p3, m3, p4, a_y)
    bc = jnp.stack([p3, p2, p1, part_bc, m1, m2, m3, p4])

    b_0, c_0 = bc[:, : FLAT[1]], bc[:, FLAT[1] :]
    b_1, b_3 = turn(b_0, "x", 1), turn(b_0, "x", -1)
    c_1, c_3 = shift(c_0, "y", 1), shift(c_0, "y", -1)
    a_x = jnp.stack([a_y, trade(a_y, "x", 1)])
    b_1, b_3, c_1, c_3, a_x = together(b_1, b_3, c_1, c_3, a_x)
    b_2 = turn(b_1[:4], "x", 1), turn(b_3[4:], "x", -1)
    c_2 = shift(c_1[:4], "y", 1), shift(c_3[4:], "y", -1)
    a_x = jnp.concatenate([a_x, trade(a_x, "x", 2)], axis=0)
    *b_2, c_20, c_21, a_x = together(*b_2, *c_2, a_x)
    b_x = jnp.stack([b_0, b_1, jnp.concatenate(b_2, axis=0), b_3])
    c_y = jnp.concatenate([c_0, c_1, jnp.concatenate([c_20, c_21], axis=0), c_3], axis=1)

    own = mixing(owner_map, couple_type, couple_multipole, couple_angle, angular)

    a_z = lax.all_gather(a_x, "z", axis=0, tiled=False)
    y_1, y_3 = shift(b_x, "y", 1), shift(b_x, "y", -1)
    x_1, x_3 = turn(c_y, "x", 1), turn(c_y, "x", -1)
    other = lax.ppermute(own, "core", [(0, 1), (1, 0)])
    y_1, y_3, x_1, x_3, other = together(y_1, y_3, x_1, x_3, other)
    y_2 = shift(y_1[:2], "y", 1), shift(y_3[2:], "y", -1)
    x_2 = turn(x_1[:4], "x", 1), turn(x_3[4:], "x", -1)
    *y_2, x_20, x_21 = together(*y_2, *x_2)
    x_2 = x_20, x_21

    b_parts = [b_x, y_1, *y_2, y_3]
    out = None
    received = []
    for steps, c_parts in (((0, 1, 3), (c_y, x_1, x_3)), ((2,), x_2)):
        out, given = product(steps, own, other, a_z, b_parts, c_parts, out)
        received.append(lax.ppermute(given, "core", [(0, 1), (1, 0)]))
    out = place((0, 1, 3), received[0], out)
    return place((2,), received[1], out)


def solution(mesh):
    fine = Mesh(mesh.devices.reshape(NY, NC, NX, NZ), ("y", "core", "x", "z"))
    groups = ("y", "core")
    return jax.shard_map(
        body,
        mesh=fine,
        in_specs=(
            P(groups, None, ("x", "z"), None),
            P(groups, None),
            P(groups, None),
            P(groups, None),
            P(),
            P(groups),
        ),
        out_specs=P(("y", "core", "x", "z"), None, None),
        check_vma=False,
    )
```
